32 devices in a mesh: ep: 16 (over z, x, core), rep: 2 (over y).
Axes of the slice: x: 2, y: 2, z: 4, core: 2. Of those that a mesh axis runs over, the one named last changes fastest.
Arguments:
- tokens_one: bfloat16 [512, 7168], P('ep', 'rep'), may hold values from -6 to 6
- tokens_two: bfloat16 [512, 7168], P('ep', 'rep'), may hold values from -6 to 6
- routes_one: int32 [512, 8], P('ep'), may hold values from 0 to 15, all different within a row; in each aligned block of 32 rows (0 to 31, 32 to 63, ...) at most 32 rows name the same one
- routes_two: int32 [512, 8], P('ep'), may hold values from 0 to 15, all different within a row; in each aligned block of 32 rows (0 to 31, 32 to 63, ...) at most 32 rows name the same one
- gates_one: float32 [512, 8], P('ep'), may hold values from 0.1 to 0.6
- gates_two: float32 [512, 8], P('ep'), may hold values from 0.1 to 0.6
- place_before: int32 [16], replicated, may hold values from 0 to 15, each once
- swap_flags: int32 [8], replicated, may hold values 0 or 1
- gate_weight: bfloat16 [16, 7168, 1024], P('ep', 'rep'), may hold values from -0.0625 to 0.0625
- up_weight: bfloat16 [16, 7168, 1024], P('ep', 'rep'), may hold values from -0.0625 to 0.0625
- down_weight: bfloat16 [16, 1024, 7168], P('ep', None, 'rep'), may hold values from -0.1875 to 0.1875
Outputs:
- mixed_one: bfloat16 [512, 7168], P('ep', 'rep')
- mixed_two: bfloat16 [512, 7168], P('ep', 'rep')
The draws below stay inside these ranges and needn't reach their ends.
Inputs may be any that keep to these rules, and one draw needn't show every extreme that they name: `routes_one`: in each aligned block of 32 rows (the rows of one index of ep) no expert is named more than 32 times, and in every draw some expert is named exactly 32 times in some block; a row names 8 different experts. `routes_two`: in each aligned block of 32 rows (the rows of one index of ep) no ep index is named more than 32 times, and in every draw some is named exactly 32 times in some block; a row names 8 different ep indices. `place_before`: each ep index appears once.
All inputs are finite; a program needn't handle non-finite values.
Results may differ from the reference program's by a relative error of at most 0.0058.
Values may be sent and summed in bfloat16 or wider, within the bound.
No kernel may reach another device: no remote copies, remote signals or barrier semaphores. Data moves between devices by JAX's collectives and lax.ppermute only.
A program may use at most 128 MiB of HBM per device.

```python
import math
import jax
import jax.numpy as jnp
import numpy as np
from jax import lax

D = 7168
FH = 1024
TOP = 8
R_EP = 32
MOST = 32
EXPERTS = 16
HALF = 8
TOKENS = 512
N_EP = 16


def place_ends(result, rng, least, largest):
    place = [jax.random.randint(jax.random.fold_in(rng, axis), (), 0, length) for axis, length in enumerate(result.shape)]
    longest = result.shape.index(max(result.shape))
    beside = place[:longest] + [(place[longest] + 1) % result.shape[longest]] + place[longest + 1:]
    return result.at[tuple(place)].set(least).at[tuple(beside)].set(largest)


def level_of(stream_key, shape, shards, least, high):
    gain = 1.0
    for position, blocks in shards:
        heights = jax.random.uniform(jax.random.fold_in(jax.random.fold_in(stream_key, 6), position), (blocks,), jnp.float32, least / len(shards), high / len(shards))
        gain = gain * jnp.repeat(jnp.exp(heights), shape[position] // blocks).reshape((-1,) + (1,) * (len(shape) - 1 - position))
    return gain


def deal_out(rng, own, number, rows, count, top, reach, slope):
    sequence = jax.random.permutation(rng, count)
    packed, usual = load_shares(count, rows * top, reach, slope, True), load_shares(count, rows * top, reach, slope, False)
    places = jnp.arange(count)

    def named(tallies, rotation):
        used = int((tallies > 0).sum())
        fixed = max(1, used // 4)
        shifted = fixed + (places - fixed + rotation * (used - fixed)) % max(1, count - fixed)
        return jnp.zeros((count,), jnp.int32).at[sequence[jnp.where(places < fixed, places, shifted)]].set(jnp.asarray(tallies, jnp.int32))

    tallies = jnp.where(number % 4 == 0, named(packed, number // 4), named(usual, number - number // 4 - 1))
    mixed = jax.random.permutation(jax.random.fold_in(own, 3), count)
    giver, receiver = mixed[0:count // 2 * 2:2], mixed[1:count // 2 * 2:2]
    margin = jnp.minimum(tallies[giver] - 1, reach - tallies[receiver]) // 2
    margin = jnp.where((giver == sequence[0]) | (receiver == sequence[0]) | (tallies[receiver] == 0), 0, jnp.maximum(margin, 0))
    shifted = jax.random.randint(jax.random.fold_in(own, 4), (count // 2,), 0, 1 << 20) % (margin + 1)
    tallies = tallies.at[giver].add(-shifted).at[receiver].add(shifted)
    labels = jnp.searchsorted(jnp.cumsum(tallies), jnp.arange(rows * top), side="right").astype(jnp.int32)
    listing = labels.reshape(top, rows).T
    listing = listing[jax.random.permutation(jax.random.fold_in(own, 1), rows)]
    rotation = jax.random.randint(jax.random.fold_in(own, 2), (rows, 1), 0, top)
    return jnp.take_along_axis(listing, (jnp.arange(top)[None, :] + rotation) % top, axis=1)


def load_shares(count, total, most, lean, full):
    loads = [(1 << 20) // math.isqrt(rank ** lean) + 1 for rank in range(1, count + 1)]
    largest = most if full else min(most, max(-(-total // count), total * loads[0] // sum(loads)))
    least = 1 if total - largest >= count - 1 else 0
    counts, spare = [largest] + [least] * (count - 1), total - largest - least * (count - 1)
    while spare > 0:
        movable = [i for i in range(1, count) if counts[i] < largest] or [i for i in range(1, count) if counts[i] < most]
        pool, left = sum([loads[i] for i in movable]), spare
        for i in movable:
            extra = min(most - counts[i], max(1, left * loads[i] // pool), spare)
            counts[i] = counts[i] + extra
            spare = spare - extra
    return np.array(counts)


def centred(rng, shape, scale, bound, shards=(), held_as=jnp.bfloat16):
    gain = level_of(rng, shape, shards, -0.22, 0.18) if shards else 1.0
    entries = jax.random.normal(rng, shape, jnp.float32) * scale * gain
    return jnp.minimum(jnp.maximum(entries, -bound), bound).astype(held_as)


def setup_inputs(seed: int = 0) -> dict:
    arg_keys = jax.random.split(jax.random.key(seed), 12)
    tokens_one = centred(arg_keys[0], (TOKENS, D), 1.0, 6.0, ((0, 16), (1, 2)))
    tokens_two = centred(arg_keys[1], (TOKENS, D), 1.0, 6.0, ((0, 16), (1, 2)))
    routes_one_keys = jax.random.split(jax.random.fold_in(arg_keys[2], 1), TOKENS // R_EP)
    routes_one_turns = jax.random.permutation(jax.random.fold_in(arg_keys[2], 3), TOKENS // R_EP)
    routes_one = jax.vmap(lambda own, number: deal_out(jax.random.fold_in(arg_keys[2], 2), own, number, R_EP, N_EP, TOP, MOST, 2))(routes_one_keys, routes_one_turns).reshape((TOKENS, TOP))
    routes_two_keys = jax.random.split(jax.random.fold_in(arg_keys[3], 1), TOKENS // R_EP)
    routes_two_turns = jax.random.permutation(jax.random.fold_in(arg_keys[3], 3), TOKENS // R_EP)
    routes_two = jax.vmap(lambda own, number: deal_out(jax.random.fold_in(arg_keys[3], 2), own, number, R_EP, N_EP, TOP, MOST, 2))(routes_two_keys, routes_two_turns).reshape((TOKENS, TOP))
    gates_one = jnp.clip(0.1 + 0.5 * jax.random.uniform(arg_keys[4], (TOKENS, TOP), jnp.float32) ** level_of(arg_keys[4], (TOKENS, TOP), ((0, 16),), -0.2, 0.2), 0.1, 0.6)
    gates_two = jnp.clip(0.1 + 0.5 * jax.random.uniform(arg_keys[5], (TOKENS, TOP), jnp.float32) ** level_of(arg_keys[5], (TOKENS, TOP), ((0, 16),), -0.2, 0.2), 0.1, 0.6)
    place_before = jax.random.permutation(arg_keys[6], N_EP).astype(jnp.int32)
    swap_flags = place_ends((jax.random.randint(arg_keys[7], (HALF,), 0, 2) < 1).astype(jnp.int32), jax.random.fold_in(arg_keys[7], 1), 0, 1)
    gate_weight = centred(arg_keys[8], (EXPERTS, D, FH), D ** -0.5, 0.0625, ((0, 16), (1, 2)))
    up_weight = centred(arg_keys[9], (EXPERTS, D, FH), D ** -0.5, 0.0625, ((0, 16), (1, 2)))
    down_weight = centred(arg_keys[10], (EXPERTS, FH, D), FH ** -0.5, 0.1875, ((0, 16), (2, 2)))
    return dict(tokens_one=tokens_one, tokens_two=tokens_two, routes_one=routes_one, routes_two=routes_two, gates_one=gates_one, gates_two=gates_two, place_before=place_before, swap_flags=swap_flags, gate_weight=gate_weight, up_weight=up_weight, down_weight=down_weight)


def expert_rows(row_block, gate_mat, up_mat, down_mat):
    gate_val = jnp.dot(row_block, gate_mat, preferred_element_type=jnp.float32)
    up_val = jnp.dot(row_block, up_mat, preferred_element_type=jnp.float32)
    hidden = (jax.nn.silu(gate_val) * up_val).astype(jnp.bfloat16)
    return jnp.dot(hidden, down_mat, preferred_element_type=jnp.float32).astype(jnp.bfloat16)


def mixture(tokens, slots, gates, gate_weight, up_weight, down_weight, source_slot):
    capacity = N_EP * MOST

    def add_slot(running, slot_id):
        is_named = slots == slot_id
        is_used = jnp.any(is_named, axis=1)
        row_index = jnp.nonzero(is_used, size=capacity, fill_value=0)[0].astype(jnp.int32)
        is_valid = jnp.arange(capacity) < jnp.sum(is_used.astype(jnp.int32))
        holder = source_slot[slot_id]
        expert_out = expert_rows(tokens[row_index], gate_weight[holder], up_weight[holder], down_weight[holder])
        weight = jnp.sum(jnp.where(is_named[row_index], gates[row_index], 0.0), axis=1)
        weight = jnp.where(is_valid, weight, 0.0)
        running = running.at[row_index].add(weight[:, None] * expert_out.astype(jnp.float32))
        return running, None

    initial = jnp.zeros((tokens.shape[0], tokens.shape[1]), jnp.float32)
    running, unused = lax.scan(add_slot, initial, jnp.arange(EXPERTS, dtype=jnp.int32))
    return running.astype(jnp.bfloat16)


def reference(tokens_one, tokens_two, routes_one, routes_two, gates_one, gates_two, place_before, swap_flags, gate_weight, up_weight, down_weight):
    indices = jnp.arange(EXPERTS, dtype=jnp.int32)
    slots_one = jnp.take(place_before, routes_one, axis=0)
    mixed_one = mixture(tokens_one, slots_one, gates_one, gate_weight, up_weight, down_weight, indices)
    partner = jnp.where(indices < HALF, indices + HALF, indices - HALF)
    flagged = jnp.take(swap_flags, indices % HALF, axis=0) == 1
    source_two = jnp.where(flagged, partner, indices)
    mixed_two = mixture(tokens_two, routes_two, gates_two, gate_weight, up_weight, down_weight, source_two)
    return mixed_one, mixed_two
```

```python
import functools

import jax
import jax.numpy as jnp
from jax import lax
from jax.experimental import pallas as pl
from jax.experimental.pallas import tpu as pltpu
from jax.sharding import PartitionSpec as P

VMEM_LIMIT = 48 * 1024 * 1024
F32 = jnp.float32
BF16 = jnp.bfloat16


def partial_kernel(part_ref, x_ref, gate_ref, up_ref, out_ref):
    rows = x_ref[...]
    out_ref[0] = jnp.dot(rows, gate_ref[...], preferred_element_type=F32).astype(out_ref.dtype)
    out_ref[1] = jnp.dot(rows, up_ref[...], preferred_element_type=F32).astype(out_ref.dtype)


def partial_sums(rows, gate_weight, up_weight, part, part_width, dtype):
    count, depth = rows.shape
    tile = min(256, part_width)
    tiles = part_width // tile
    weight_spec = pl.BlockSpec((None, depth, tile), lambda j, part_ref: (0, 0, part_ref[0] * tiles + j))
    return pl.pallas_call(
        partial_kernel,
        out_shape=jax.ShapeDtypeStruct((2, count, part_width), dtype),
        grid_spec=pltpu.PrefetchScalarGridSpec(
            num_scalar_prefetch=1,
            grid=(tiles,),
            in_specs=[pl.BlockSpec((count, depth), lambda j, part_ref: (0, 0)), weight_spec, weight_spec],
            out_specs=pl.BlockSpec((2, count, tile), lambda j, part_ref: (0, 0, j)),
        ),
        compiler_params=pltpu.CompilerParams(vmem_limit_bytes=VMEM_LIMIT),
        cost_estimate=pl.CostEstimate(
            flops=4 * count * depth * part_width,
            bytes_accessed=2 * (count * depth + 2 * depth * part_width + 2 * count * part_width),
            transcendentals=0,
        ),
    )(part.reshape(1), rows, gate_weight, up_weight)


def down_kernel(parts, index_ref, *refs):
    hidden_refs = refs[:parts]
    down_refs = refs[parts : 2 * parts]
    scale_ref, own_ref, sent_ref = refs[2 * parts :]
    core = index_ref[0]
    groups, _, rows, width = hidden_refs[0].shape
    tile = own_ref.shape[-1]
    for side, out_ref in ((1 - core, sent_ref), (core, own_ref)):
        total = None
        for hidden_ref, down_ref in zip(hidden_refs, down_refs):
            block = hidden_ref[:, pl.ds(side, 1)].reshape(groups * rows, width)
            term = jnp.dot(block, down_ref[...], preferred_element_type=F32)
            total = term if total is None else total + term
        scale = scale_ref[:, pl.ds(side, 1)].reshape(groups * rows, 1)
        out_ref[...] = (total * scale).reshape(groups, rows, tile).astype(out_ref.dtype)


def down_rows(hidden_parts, down_weight, scale, core, part_ids):
    parts = len(hidden_parts)
    groups, _, rows, part_width = hidden_parts[0].shape
    width = down_weight.shape[2]
    tile = 512 if width % 512 == 0 else 256
    whole = lambda j, index_ref: (0, 0, 0, 0)
    hidden_spec = pl.BlockSpec((groups, 2, rows, part_width), whole)
    down_specs = [
        pl.BlockSpec((None, part_width, tile), functools.partial(lambda p, j, index_ref: (0, index_ref[1 + p], j), p))
        for p in range(parts)
    ]
    out_spec = pl.BlockSpec((groups, rows, tile), lambda j, index_ref: (0, 0, j))
    count = groups * 2 * rows
    return pl.pallas_call(
        functools.partial(down_kernel, parts),
        out_shape=(
            jax.ShapeDtypeStruct((groups, rows, width), F32),
            jax.ShapeDtypeStruct((groups, rows, width), BF16),
        ),
        grid_spec=pltpu.PrefetchScalarGridSpec(
            num_scalar_prefetch=1,
            grid=(width // tile,),
            in_specs=[hidden_spec] * parts + down_specs + [pl.BlockSpec((groups, 2, rows, 1), whole)],
            out_specs=(out_spec, out_spec),
        ),
        compiler_params=pltpu.CompilerParams(vmem_limit_bytes=VMEM_LIMIT),
        cost_estimate=pl.CostEstimate(
            flops=2 * count * parts * part_width * width,
            bytes_accessed=2 * parts * part_width * (width + count) + 3 * count * width,
            transcendentals=0,
        ),
    )(jnp.stack([core] + part_ids), *hidden_parts, *([down_weight] * parts), scale)


def shifted(value, axis, size, step):
    return lax.ppermute(value, axis, [(i, (i + step) % size) for i in range(size)])


def flipped(value, size, bit):
    return lax.ppermute(value, "ep", [(i, i ^ bit) for i in range(size)])


def expert_step(tokens, scale, gate_weight, up_weight, down_weight):
    ep = lax.axis_size("ep")
    rep = lax.axis_size("rep")
    me = lax.axis_index("ep")
    y = lax.axis_index("rep")
    row_count, width = tokens.shape
    core = me % 2
    x = (me // 2) % 2
    z = me // 4
    z_count = ep // 4
    part_width = gate_weight.shape[2] // rep

    rows = lax.all_gather(tokens, "ep", axis=0, tiled=True)

    sent = []
    for step in range(1, rep):
        partial = partial_sums(rows, gate_weight, up_weight, (y + step) % rep, part_width, BF16)
        sent.append(shifted(partial, "rep", rep, step))
    own = partial_sums(rows, gate_weight, up_weight, y, part_width, F32)
    for arrived in sent:
        own = own + arrived.astype(F32)
    hidden = (jax.nn.silu(own[0]) * own[1]).astype(BF16)
    hidden = hidden.reshape(z_count * 2, 2, row_count, part_width)
    hidden_parts = [hidden] + [shifted(hidden, "rep", rep, step) for step in range(1, rep)]
    part_ids = [y] + [(y - step) % rep for step in range(1, rep)]

    own_rows, sent_rows = down_rows(hidden_parts, down_weight, scale, core, part_ids)

    arrived = flipped(sent_rows, ep, 1)
    arrived = arrived.reshape(z_count, 2, row_count, width)
    own_rows = own_rows.reshape(z_count, 2, row_count, width)
    pick = lambda value, index: lax.dynamic_index_in_dim(value, index, 1, keepdims=False)
    far = (pick(own_rows, 1 - x) + pick(arrived, 1 - x).astype(F32)).astype(BF16)
    near = pick(own_rows, x) + pick(arrived, x).astype(F32)
    near = near + flipped(far, ep, 2).astype(F32)
    near_sent = near.astype(BF16)
    total = lax.dynamic_index_in_dim(near, z, 0, keepdims=False)
    for step in range(1, z_count):
        to_index = (z + step) % z_count
        block = lax.dynamic_index_in_dim(near_sent, to_index, 0, keepdims=False)
        total = total + shifted(block, "ep", ep, 4 * step).astype(F32)
    return total.astype(BF16)


def shards(
    tokens_one,
    tokens_two,
    routes_one,
    routes_two,
    gates_one,
    gates_two,
    place_before,
    swap_flags,
    gate_weight,
    up_weight,
    down_weight,
):
    ep = lax.axis_size("ep")
    half = ep // 2
    me = lax.axis_index("ep")
    row_count = tokens_one.shape[0]
    indices = jnp.arange(ep, dtype=jnp.int32)
    slots_one = jnp.sum(jnp.where(routes_one[:, :, None] == indices, place_before, 0), axis=2)
    partner = jnp.where(indices < half, indices + half, indices - half)
    flagged = jnp.concatenate([swap_flags, swap_flags]) == 1
    source_two = jnp.where(flagged, partner, indices)
    slots_two = jnp.sum(jnp.where(routes_two[:, :, None] == indices, source_two, 0), axis=2)

    def shares(slots, gates):
        return jnp.sum(jnp.where(slots[:, :, None] == indices, gates[:, :, None], 0.0), axis=1)

    mine = jnp.stack([shares(slots_one, gates_one), shares(slots_two, gates_two)])
    shares_all = lax.all_gather(mine, "ep")
    scales = lax.dynamic_index_in_dim(shares_all, me, 3, keepdims=True)
    scales = scales.reshape(half, 2, 2, row_count, 1)

    mixed_one = expert_step(tokens_one, scales[:, :, 0], gate_weight, up_weight, down_weight)
    mixed_two = expert_step(tokens_two, scales[:, :, 1], gate_weight, up_weight, down_weight)
    return (mixed_one, mixed_two)


def solution(mesh):
    return jax.shard_map(
        shards,
        mesh=mesh,
        in_specs=(
            P("ep", "rep"),
            P("ep", "rep"),
            P("ep", None),
            P("ep", None),
            P("ep", None),
            P("ep", None),
            P(),
            P(),
            P("ep", "rep", None),
            P("ep", "rep", None),
            P("ep", None, "rep"),
        ),
        out_specs=(P("ep", "rep"), P("ep", "rep")),
        check_vma=False,
    )
```

```python
import functools

import jax
import jax.numpy as jnp
from jax import lax
from jax.experimental import pallas as pl
from jax.experimental.pallas import tpu as pltpu
from jax.sharding import PartitionSpec as P

VMEM_LIMIT = 56 * 1024 * 1024
F32 = jnp.float32
BF16 = jnp.bfloat16
EXTRA = 128
PIECES = 3


def sums_kernel(block_count, arrived_count, part_ref, *refs):
    row_refs = refs[:block_count]
    gate_ref, up_ref = refs[block_count : block_count + 2]
    arrived_refs = refs[block_count + 2 : block_count + 2 + arrived_count]
    out_ref, total = refs[block_count + 2 + arrived_count :]
    step = pl.program_id(0)
    rows = jnp.concatenate([ref[...] for ref in row_refs], axis=0)
    gate = jnp.dot(rows, gate_ref[...], preferred_element_type=F32)
    up = jnp.dot(rows, up_ref[...], preferred_element_type=F32)

    @pl.when(step == 0)
    def _():
        total[0] = gate
        total[1] = up

    @pl.when(step > 0)
    def _():
        total[0] += gate
        total[1] += up

    @pl.when(step == pl.num_programs(0) - 1)
    def _():
        if len(out_ref.shape) == 3:
            out_ref[...] = total[...].astype(out_ref.dtype)
        else:
            gate_sum, up_sum = total[0], total[1]
            for ref in arrived_refs:
                gate_sum = gate_sum + ref[0].astype(F32)
                up_sum = up_sum + ref[1].astype(F32)
            out_ref[...] = (gate_sum / (1.0 + jnp.exp(-gate_sum)) * up_sum).astype(out_ref.dtype)


def sums(blocks, gate_weight, up_weight, part, part_width, arrived):
    block_rows = blocks[0].shape[0]
    count = block_rows * len(blocks)
    depth = gate_weight.shape[1]
    tile = 512 if depth % 512 == 0 else 256
    finish = arrived is not None
    arrived = arrived or []
    row_spec = pl.BlockSpec((block_rows, tile), lambda k, part_ref: (0, k))
    weight_spec = pl.BlockSpec((None, tile, part_width), lambda k, part_ref: (0, k, part_ref[0]))
    pair_spec = pl.BlockSpec((2, count, part_width), lambda k, part_ref: (0, 0, 0))
    out_spec = pl.BlockSpec((count, part_width), lambda k, part_ref: (0, 0)) if finish else pair_spec
    out_shape = (count, part_width) if finish else (2, count, part_width)
    return pl.pallas_call(
        functools.partial(sums_kernel, len(blocks), len(arrived)),
        out_shape=jax.ShapeDtypeStruct(out_shape, BF16),
        grid_spec=pltpu.PrefetchScalarGridSpec(
            num_scalar_prefetch=1,
            grid=(depth // tile,),
            in_specs=[row_spec] * len(blocks) + [weight_spec] * 2 + [pair_spec] * len(arrived),
            out_specs=out_spec,
            scratch_shapes=[pltpu.VMEM((2, count, part_width), F32)],
        ),
        compiler_params=pltpu.CompilerParams(vmem_limit_bytes=VMEM_LIMIT),
        cost_estimate=pl.CostEstimate(
            flops=4 * count * depth * part_width,
            bytes_accessed=2 * (count * depth + 2 * depth * part_width + 2 * count * part_width),
            transcendentals=count * part_width if finish else 0,
        ),
    )(part.reshape(1), *blocks, gate_weight, up_weight, *arrived)


def down_kernel(parts, block_count, step_rows, scalar_ref, *refs):
    hidden_refs = refs[:parts]
    down_refs = refs[parts : 2 * parts]
    extra_refs = refs[2 * parts : 2 * parts + block_count]
    own_ref, sent_ref = refs[2 * parts + block_count :]
    scales = []
    for ref in extra_refs:
        values = ref[...].astype(F32)
        names = pltpu.roll(values, EXTRA // 2, 1)
        row = lax.broadcasted_iota(jnp.int32, values.shape, 0)
        lane = lax.broadcasted_iota(jnp.int32, values.shape, 1)
        wanted = jnp.where(row < step_rows, scalar_ref[0], scalar_ref[1]).astype(F32)
        chosen = jnp.logical_and(names == wanted, lane < EXTRA // 2)
        scales.append(jnp.sum(jnp.where(chosen, values, 0.0), axis=1, keepdims=True))
    scale = jnp.concatenate(scales, axis=0)
    total = None
    for hidden_ref, down_ref in zip(hidden_refs, down_refs):
        term = jnp.dot(hidden_ref[...], down_ref[...], preferred_element_type=F32)
        total = term if total is None else total + term
    total = total * scale
    middle = total.shape[0] // 2
    own_ref[...] = total[:middle]
    sent_ref[...] = total[middle:].astype(sent_ref.dtype)


def down_rows(hidden_parts, down_weight, blocks, step_rows, wanted, part_ids):
    parts = len(hidden_parts)
    count, part_width = hidden_parts[0].shape
    width = down_weight.shape[2]
    block_rows = blocks[0].shape[0]
    tile = 512 if width % 512 == 0 else 256
    hidden_spec = pl.BlockSpec((count, part_width), lambda j, ref: (0, 0))
    down_specs = [
        pl.BlockSpec((None, part_width, tile), functools.partial(lambda p, j, ref: (0, ref[2 + p], j), p))
        for p in range(parts)
    ]
    extra_spec = pl.BlockSpec((block_rows, EXTRA), lambda j, ref: (0, width // EXTRA))
    out_spec = pl.BlockSpec((count // 2, tile), lambda j, ref: (0, j))
    return pl.pallas_call(
        functools.partial(down_kernel, parts, len(blocks), step_rows),
        out_shape=(
            jax.ShapeDtypeStruct((count // 2, width), F32),
            jax.ShapeDtypeStruct((count // 2, width), BF16),
        ),
        grid_spec=pltpu.PrefetchScalarGridSpec(
            num_scalar_prefetch=1,
            grid=(width // tile,),
            in_specs=[hidden_spec] * parts + down_specs + [extra_spec] * len(blocks),
            out_specs=(out_spec, out_spec),
        ),
        compiler_params=pltpu.CompilerParams(vmem_limit_bytes=VMEM_LIMIT),
        cost_estimate=pl.CostEstimate(
            flops=2 * count * parts * part_width * width,
            bytes_accessed=2 * parts * part_width * (width + count) + 3 * count * width,
            transcendentals=0,
        ),
    )(jnp.stack(wanted + part_ids), *hidden_parts, *([down_weight] * parts), *blocks)


def shifted(value, axis, size, step):
    return lax.ppermute(value, axis, [(i, (i + step) % size) for i in range(size)])


def flipped(value, size, bits):
    return lax.ppermute(value, "ep", [(i, i ^ bits) for i in range(size)])


def extras(routes, gates):
    top = gates.shape[1]
    columns = []
    rest = gates
    for _ in range(PIECES):
        piece = lax.reduce_precision(rest, 8, 7)
        columns.append(piece)
        rest = rest - piece
    values = jnp.pad(jnp.concatenate(columns, axis=1), ((0, 0), (0, EXTRA // 2 - PIECES * top)))
    names = jnp.pad(jnp.concatenate([routes] * PIECES, axis=1), ((0, 0), (0, EXTRA // 2 - PIECES * top)))
    return jnp.concatenate([values, names.astype(F32)], axis=1).astype(BF16)


def shards(
    tokens_one,
    tokens_two,
    routes_one,
    routes_two,
    gates_one,
    gates_two,
    place_before,
    swap_flags,
    gate_weight,
    up_weight,
    down_weight,
):
    ep = lax.axis_size("ep")
    rep = lax.axis_size("rep")
    me = lax.axis_index("ep")
    y = lax.axis_index("rep")
    half = ep // 2
    z_count = ep // 4
    row_count, width = tokens_one.shape
    part_width = gate_weight.shape[2] // rep
    indices = jnp.arange(ep, dtype=jnp.int32)

    expert = jnp.sum(jnp.where(place_before == me, indices, 0))
    flag = jnp.sum(jnp.where(indices[:half] == me % half, swap_flags, 0))
    after = jnp.where(flag == 1, jnp.where(me < half, me + half, me - half), me)
    wanted = [expert, after]

    both = jnp.concatenate(
        [
            jnp.concatenate([tokens_one, extras(routes_one, gates_one)], axis=1),
            jnp.concatenate([tokens_two, extras(routes_two, gates_two)], axis=1),
        ],
        axis=0,
    )

    order = list(range(z_count))
    along_z = {r: both if r == 0 else flipped(both, ep, 4 * r) for r in order}
    groups = min(4, z_count)
    per_group = z_count // groups
    own_sums, finals = {}, None
    part_ids = [y] + [(y - step) % rep for step in range(1, rep)]
    total = None
    sent_z = []
    for group in range(groups):
        members = order[group * per_group : (group + 1) * per_group]
        near = [along_z[r] for r in members]
        across = [flipped(value, ep, 2) for value in near]
        blocks = near + across
        blocks = blocks + [flipped(value, ep, 1) for value in blocks]
        arrived = []
        for step in range(1, rep):
            partial = sums(blocks, gate_weight, up_weight, (y + step) % rep, part_width, None)
            arrived.append(shifted(partial, "rep", rep, step))
        hidden = sums(blocks, gate_weight, up_weight, y, part_width, arrived)
        hidden_parts = [hidden] + [shifted(hidden, "rep", rep, step) for step in range(1, rep)]
        own_rows, sent_rows = down_rows(hidden_parts, down_weight, blocks, row_count, wanted, part_ids)
        by_core = own_rows + flipped(sent_rows, ep, 1).astype(F32)
        middle = by_core.shape[0] // 2
        by_x = by_core[:middle] + flipped(by_core[middle:].astype(BF16), ep, 2).astype(F32)
        by_x = by_x.reshape(per_group, 2 * row_count, width)
        for place, r in enumerate(members):
            block = by_x[place] if r == 0 else flipped(by_x[place].astype(BF16), ep, 4 * r).astype(F32)
            total = block if total is None else total + block
    return total[:row_count].astype(BF16), total[row_count:].astype(BF16)


def solution(mesh):
    return jax.shard_map(
        shards,
        mesh=mesh,
        in_specs=(
            P("ep", "rep"),
            P("ep", "rep"),
            P("ep", None),
            P("ep", None),
            P("ep", None),
            P("ep", None),
            P(),
            P(),
            P("ep", "rep", None),
            P("ep", "rep", None),
            P("ep", None, "rep"),
        ),
        out_specs=(P("ep", "rep"), P("ep", "rep")),
        check_vma=False,
    )
```

```python
import functools

import jax
import jax.numpy as jnp
from jax import lax
from jax.experimental import pallas as pl
from jax.experimental.pallas import tpu as pltpu
from jax.sharding import PartitionSpec as P

VMEM_LIMIT = 56 * 1024 * 1024
F32 = jnp.float32
BF16 = jnp.bfloat16
EXTRA = 128
PIECES = 3


def scale_of(extra, step_rows, one, two):
    values = extra.astype(F32)
    names = pltpu.roll(values, EXTRA // 2, 1)
    row = lax.broadcasted_iota(jnp.int32, values.shape, 0)
    lane = lax.broadcasted_iota(jnp.int32, values.shape, 1)
    wanted = jnp.where(row < step_rows, one, two).astype(F32)
    chosen = jnp.logical_and(names == wanted, lane < EXTRA // 2)
    return jnp.sum(jnp.where(chosen, values, 0.0), axis=1, keepdims=True)


def sums_kernel(block_count, arrived_count, after_count, part_ref, *refs):
    block_refs = refs[:block_count]
    gate_ref, up_ref = refs[block_count : block_count + 2]
    arrived_refs = refs[block_count + 2 : block_count + 2 + arrived_count]
    refs = refs[block_count + 2 + arrived_count + after_count :]
    out_ref, rows, gates, ups, total, row_sems, gate_sems, up_sems = refs
    steps, tile, part_width = gates.shape
    block_rows = block_refs[0].shape[0]
    depth = steps * tile
    columns = pl.ds(pl.multiple_of(part_ref[0] * part_width, part_width), part_width)
    row_copies = [
        pltpu.make_async_copy(
            ref.at[:, pl.ds(0, depth)], rows.at[pl.ds(i * block_rows, block_rows)], row_sems.at[i]
        )
        for i, ref in enumerate(block_refs)
    ]
    weight_copies = []
    for step in range(steps):
        span = pl.ds(step * tile, tile)
        weight_copies.append(
            (
                pltpu.make_async_copy(gate_ref.at[0, span, columns], gates.at[step], gate_sems.at[step]),
                pltpu.make_async_copy(up_ref.at[0, span, columns], ups.at[step], up_sems.at[step]),
            )
        )
    for copy in row_copies:
        copy.start()
    for pair in weight_copies:
        for copy in pair:
            copy.start()
    for copy in row_copies:
        copy.wait()
    for step, pair in enumerate(weight_copies):
        for copy in pair:
            copy.wait()
        block = rows[:, step * tile : (step + 1) * tile]
        for place, weights in enumerate((gates, ups)):
            term = jnp.dot(block, weights[step], preferred_element_type=F32)
            if step == 0:
                total[place] = term
            elif step < steps - 1:
                total[place] += term
            elif arrived_count == 0:
                out_ref[place] = (total[place] + term).astype(out_ref.dtype)
            else:
                term = total[place] + term
                for ref in arrived_refs:
                    term = term + ref[place].astype(F32)
                if place == 0:
                    gate_sum = term
                else:
                    out_ref[...] = (gate_sum / (1.0 + jnp.exp(-gate_sum)) * term).astype(out_ref.dtype)


def sums(blocks, gate_weight, up_weight, part, part_width, arrived, after):
    block_rows = blocks[0].shape[0]
    count = block_rows * len(blocks)
    depth = gate_weight.shape[1]
    tile = 512 if depth % 512 == 0 else 256
    steps = depth // tile
    out_shape = (count, part_width) if arrived else (2, count, part_width)
    any_spec = pl.BlockSpec(memory_space=pl.ANY)
    vmem_spec = pl.BlockSpec(memory_space=pltpu.VMEM)
    return pl.pallas_call(
        functools.partial(sums_kernel, len(blocks), len(arrived), len(after)),
        out_shape=jax.ShapeDtypeStruct(out_shape, BF16),
        grid_spec=pltpu.PrefetchScalarGridSpec(
            num_scalar_prefetch=1,
            grid=(),
            in_specs=[any_spec] * (len(blocks) + 2) + [vmem_spec] * len(arrived) + [any_spec] * len(after),
            out_specs=vmem_spec,
            scratch_shapes=[
                pltpu.VMEM((count, depth), BF16),
                pltpu.VMEM((steps, tile, part_width), BF16),
                pltpu.VMEM((steps, tile, part_width), BF16),
                pltpu.VMEM((2, count, part_width), F32),
                pltpu.SemaphoreType.DMA((len(blocks),)),
                pltpu.SemaphoreType.DMA((steps,)),
                pltpu.SemaphoreType.DMA((steps,)),
            ],
        ),
        compiler_params=pltpu.CompilerParams(vmem_limit_bytes=VMEM_LIMIT),
        cost_estimate=pl.CostEstimate(
            flops=4 * count * depth * part_width,
            bytes_accessed=2 * (count * depth + 2 * depth * part_width + 2 * count * part_width),
            transcendentals=count * part_width if arrived else 0,
        ),
    )(part.reshape(1), *blocks, gate_weight, up_weight, *arrived, *after)


def down_kernel(parts, block_count, after_count, step_rows, scalar_ref, *refs):
    hidden_refs = refs[:parts]
    down_ref = refs[parts]
    block_refs = refs[parts + 1 : parts + 1 + block_count]
    refs = refs[parts + 1 + block_count + after_count :]
    own_out, sent_out, weights, extra, own, sent, extra_sems, weight_sems, own_sems, sent_sems = refs
    tiles, _, part_width, tile = weights.shape
    block_rows = extra.shape[1]
    width = tiles * tile
    copies = []
    for j in range(tiles):
        for p in range(parts):
            start = pl.multiple_of(scalar_ref[2 + p] * part_width, part_width)
            copies.append(
                pltpu.make_async_copy(
                    down_ref.at[0, pl.ds(start, part_width), pl.ds(j * tile, tile)],
                    weights.at[j, p],
                    weight_sems.at[j, p],
                )
            )
    extra_copies = [
        pltpu.make_async_copy(ref.at[:, pl.ds(width, EXTRA)], extra.at[i], extra_sems.at[i])
        for i, ref in enumerate(block_refs)
    ]
    for copy in extra_copies + copies:
        copy.start()
    for copy in extra_copies:
        copy.wait()
    scale = jnp.concatenate(
        [scale_of(extra[i], step_rows, scalar_ref[0], scalar_ref[1]) for i in range(block_count)], axis=0
    )
    middle = block_count * block_rows // 2
    out_copies = []
    for j in range(tiles):
        total = None
        for p in range(parts):
            copies[j * parts + p].wait()
            term = jnp.dot(hidden_refs[p][...], weights[j, p], preferred_element_type=F32)
            total = term if total is None else total + term
        total = total * scale
        span = pl.ds(j * tile, tile)
        own[:, span] = total[:middle]
        sent[:, span] = total[middle:].astype(BF16)
        for buffer, out_ref, sems in ((sent, sent_out, sent_sems), (own, own_out, own_sems)):
            copy = pltpu.make_async_copy(buffer.at[:, span], out_ref.at[:, span], sems.at[j])
            copy.start()
            out_copies.append(copy)
    for copy in out_copies:
        copy.wait()


def down_rows(hidden_parts, down_weight, blocks, step_rows, wanted, part_ids, after):
    parts = len(hidden_parts)
    count, part_width = hidden_parts[0].shape
    width = down_weight.shape[2]
    block_rows = blocks[0].shape[0]
    tile = 512 if width % 512 == 0 else 256
    tiles = width // tile
    any_spec = pl.BlockSpec(memory_space=pl.ANY)
    vmem_spec = pl.BlockSpec(memory_space=pltpu.VMEM)
    return pl.pallas_call(
        functools.partial(down_kernel, parts, len(blocks), len(after), step_rows),
        out_shape=(
            jax.ShapeDtypeStruct((count // 2, width), F32),
            jax.ShapeDtypeStruct((count // 2, width), BF16),
        ),
        grid_spec=pltpu.PrefetchScalarGridSpec(
            num_scalar_prefetch=1,
            grid=(),
            in_specs=[vmem_spec] * parts + [any_spec] * (1 + len(blocks) + len(after)),
            out_specs=(any_spec, any_spec),
            scratch_shapes=[
                pltpu.VMEM((tiles, parts, part_width, tile), BF16),
                pltpu.VMEM((len(blocks), block_rows, EXTRA), BF16),
                pltpu.VMEM((count // 2, width), F32),
                pltpu.VMEM((count // 2, width), BF16),
                pltpu.SemaphoreType.DMA((len(blocks),)),
                pltpu.SemaphoreType.DMA((tiles, parts)),
                pltpu.SemaphoreType.DMA((tiles,)),
                pltpu.SemaphoreType.DMA((tiles,)),
            ],
        ),
        compiler_params=pltpu.CompilerParams(vmem_limit_bytes=VMEM_LIMIT),
        cost_estimate=pl.CostEstimate(
            flops=2 * count * parts * part_width * width,
            bytes_accessed=2 * parts * part_width * (width + count) + 3 * count * width,
            transcendentals=0,
        ),
    )(jnp.stack(wanted + part_ids), *hidden_parts, down_weight, *blocks, *after)


def base_kernel(one_ref, two_ref, route_one_ref, route_two_ref, gate_one_ref, gate_two_ref, out_ref):
    step_rows, width = one_ref.shape
    top = route_one_ref.shape[0]
    out_ref[:step_rows, :width] = one_ref[...]
    out_ref[step_rows:, :width] = two_ref[...]
    column = lax.broadcasted_iota(jnp.int32, (top, EXTRA), 1)
    choice = lax.broadcasted_iota(jnp.int32, (top, EXTRA), 0)

    def placed(value, start):
        where = (column == choice + start).astype(BF16)
        return lax.dot_general(
            value.astype(BF16), where, (((0,), (0,)), ((), ())), preferred_element_type=F32
        )

    for place, route_ref, gate_ref in ((0, route_one_ref, gate_one_ref), (1, route_two_ref, gate_two_ref)):
        rest = gate_ref[...]
        names = route_ref[...].astype(F32)
        total = None
        for piece in range(PIECES):
            part = rest.astype(BF16).astype(F32)
            rest = rest - part
            term = placed(part, piece * top) + placed(names, EXTRA // 2 + piece * top)
            total = term if total is None else total + term
        out_ref[place * step_rows : (place + 1) * step_rows, width:] = total.astype(BF16)


def base_rows(tokens_one, tokens_two, routes_one, routes_two, gates_one, gates_two):
    step_rows, width = tokens_one.shape
    return pl.pallas_call(
        base_kernel,
        out_shape=jax.ShapeDtypeStruct((2 * step_rows, width + EXTRA), BF16),
        in_specs=[pl.BlockSpec(memory_space=pltpu.VMEM)] * 6,
        out_specs=pl.BlockSpec(memory_space=pltpu.VMEM),
        compiler_params=pltpu.CompilerParams(vmem_limit_bytes=VMEM_LIMIT),
    )(tokens_one, tokens_two, routes_one.T, routes_two.T, gates_one.T, gates_two.T)


def shifted(value, axis, size, step):
    return lax.ppermute(value, axis, [(i, (i + step) % size) for i in range(size)])


def flipped(value, size, bits):
    return lax.ppermute(value, "ep", [(i, i ^ bits) for i in range(size)])


def shards(
    tokens_one,
    tokens_two,
    routes_one,
    routes_two,
    gates_one,
    gates_two,
    place_before,
    swap_flags,
    gate_weight,
    up_weight,
    down_weight,
):
    ep = lax.axis_size("ep")
    rep = lax.axis_size("rep")
    me = lax.axis_index("ep")
    y = lax.axis_index("rep")
    half = ep // 2
    z_count = ep // 4
    row_count, width = tokens_one.shape
    part_width = gate_weight.shape[2] // rep
    indices = jnp.arange(ep, dtype=jnp.int32)

    expert = jnp.sum(jnp.where(place_before == me, indices, 0))
    flag = jnp.sum(jnp.where(indices[:half] == me % half, swap_flags, 0))
    after = jnp.where(flag == 1, jnp.where(me < half, me + half, me - half), me)
    wanted = [expert, after]

    both = base_rows(tokens_one, tokens_two, routes_one, routes_two, gates_one, gates_two)
    part_ids = [y] + [(y - step) % rep for step in range(1, rep)]

    groups = min(4, z_count)
    per_group = z_count // groups
    members = [[group * per_group + i for i in range(per_group)] for group in (0, 2, 3, 1)[:groups]]
    along_z = [[both if r == 0 else flipped(both, ep, 4 * r) for r in group] for group in members]
    state = [dict() for _ in range(groups)]
    last = []

    def gather(g):
        blocks = along_z[g] + [flipped(value, ep, 2) for value in along_z[g]]
        state[g]["blocks"] = blocks + [flipped(value, ep, 1) for value in blocks]

    def send_sums(g):
        state[g]["arrived"] = []
        for step in range(1, rep):
            partial = sums(
                state[g]["blocks"], gate_weight, up_weight, (y + step) % rep, part_width, [], last
            )
            last[:] = [partial]
            state[g]["arrived"].append(shifted(partial, "rep", rep, step))

    def send_hidden(g):
        hidden = sums(state[g]["blocks"], gate_weight, up_weight, y, part_width, state[g]["arrived"], last)
        last[:] = [hidden]
        state[g]["hidden"] = [hidden] + [shifted(hidden, "rep", rep, step) for step in range(1, rep)]

    def send_core(g):
        own, sent = down_rows(
            state[g]["hidden"], down_weight, state[g]["blocks"], row_count, wanted, part_ids, last
        )
        last[:] = [sent]
        state[g]["own"], state[g]["core"] = own, flipped(sent, ep, 1)

    def send_x(g):
        own, core = state[g]["own"], state[g]["core"]
        middle = own.shape[0] // 2
        far = (own[middle:] + core[middle:].astype(F32)).astype(BF16)
        last.append(far)
        state[g]["x"] = flipped(far, ep, 2)

    def send_z(g):
        own, core = state[g]["own"], state[g]["core"]
        middle = own.shape[0] // 2
        near = own[:middle] + core[:middle].astype(F32) + state[g]["x"].astype(F32)
        near = near.reshape(per_group, 2 * row_count, width)
        state[g]["z"] = []
        for place, r in enumerate(members[g]):
            if r == 0:
                state[g]["z"].append(near[place])
            else:
                block = near[place].astype(BF16)
                last.append(block)
                state[g]["z"].append(flipped(block, ep, 4 * r))

    stages = (gather, send_sums, send_hidden, send_core, send_x, send_z)
    for turn in range(groups + len(stages) - 1):
        for stage in reversed(range(len(stages))):
            if 0 <= turn - stage < groups:
                stages[stage](turn - stage)

    total = None
    for g in range(groups):
        for block in state[g]["z"]:
            total = block.astype(F32) if total is None else total + block.astype(F32)
    return total[:row_count].astype(BF16), total[row_count:].astype(BF16)


def solution(mesh):
    return jax.shard_map(
        shards,
        mesh=mesh,
        in_specs=(
            P("ep", "rep"),
            P("ep", "rep"),
            P("ep", None),
            P("ep", None),
            P("ep", None),
            P("ep", None),
            P(),
            P(),
            P("ep", "rep", None),
            P("ep", "rep", None),
            P("ep", None, "rep"),
        ),
        out_specs=(P("ep", "rep"), P("ep", "rep")),
        check_vma=False,
    )
```

```python
import functools

import jax
import jax.numpy as jnp
from jax import lax
from jax.experimental import pallas as pl
from jax.experimental.pallas import tpu as pltpu
from jax.sharding import PartitionSpec as P

VMEM_LIMIT = 20 * 1024 * 1024
QUICK = pl.CostEstimate(flops=1, bytes_accessed=1, transcendentals=0)
F32 = jnp.float32
BF16 = jnp.bfloat16
EXTRA = 128
PIECES = 3


def scale_of(extra, step_rows, one, two):
    values = extra.astype(F32)
    names = pltpu.roll(values, EXTRA // 2, 1)
    row = lax.broadcasted_iota(jnp.int32, values.shape, 0)
    lane = lax.broadcasted_iota(jnp.int32, values.shape, 1)
    wanted = jnp.where(row < step_rows, one, two).astype(F32)
    chosen = jnp.logical_and(names == wanted, lane < EXTRA // 2)
    return jnp.sum(jnp.where(chosen, values, 0.0), axis=1, keepdims=True)


def load_kernel(count, *refs):
    sems = refs[2 * count]
    copies = [pltpu.make_async_copy(refs[i], refs[count + i], sems.at[i]) for i in range(count)]
    for copy in copies:
        copy.start()
    for copy in copies:
        copy.wait()


def load(arrays, after):
    count = len(arrays)
    any_spec = pl.BlockSpec(memory_space=pl.ANY)
    return pl.pallas_call(
        lambda *refs: load_kernel(count, *refs[:count], *refs[count + len(after) :]),
        out_shape=[pltpu.VMEM(array.shape, array.dtype) for array in arrays],
        in_specs=[any_spec] * (count + len(after)),
        out_specs=[pl.BlockSpec(memory_space=pltpu.VMEM)] * count,
        scratch_shapes=[pltpu.SemaphoreType.DMA((count,))],
        compiler_params=pltpu.CompilerParams(vmem_limit_bytes=VMEM_LIMIT),
        cost_estimate=QUICK,
    )(*arrays, *after)


def sums_kernel(block_count, arrived_count, after_count, part_ref, *refs):
    block_refs = refs[:block_count]
    gate_ref, up_ref = refs[block_count : block_count + 2]
    arrived_refs = refs[block_count + 2 : block_count + 2 + arrived_count]
    out_ref, rows = refs[block_count + 2 + arrived_count + after_count :]
    block_rows = block_refs[0].shape[0]
    depth = rows.shape[1]
    part_width = out_ref.shape[-1]
    tile = 256 if part_width % 256 == 0 else part_width
    for i, ref in enumerate(block_refs):
        rows[i * block_rows : (i + 1) * block_rows] = ref[:, :depth]
    for j in range(part_width // tile):
        span = pl.ds(pl.multiple_of(part_ref[0] * part_width + j * tile, tile), tile)
        here = slice(j * tile, (j + 1) * tile)
        gate = jnp.dot(rows[...], gate_ref[0, :, span], preferred_element_type=F32)
        up = jnp.dot(rows[...], up_ref[0, :, span], preferred_element_type=F32)
        if arrived_count == 0:
            out_ref[0, :, here] = gate.astype(out_ref.dtype)
            out_ref[1, :, here] = up.astype(out_ref.dtype)
        else:
            for ref in arrived_refs:
                gate = gate + ref[0, :, here].astype(F32)
                up = up + ref[1, :, here].astype(F32)
            out_ref[:, here] = (gate / (1.0 + jnp.exp(-gate)) * up).astype(out_ref.dtype)


def sums(blocks, gate_weight, up_weight, part, part_width, arrived, after):
    count = blocks[0].shape[0] * len(blocks)
    depth = gate_weight.shape[1]
    out_shape = (count, part_width) if arrived else (2, count, part_width)
    any_spec = pl.BlockSpec(memory_space=pl.ANY)
    vmem_spec = pl.BlockSpec(memory_space=pltpu.VMEM)
    return pl.pallas_call(
        functools.partial(sums_kernel, len(blocks), len(arrived), len(after)),
        out_shape=jax.ShapeDtypeStruct(out_shape, BF16),
        grid_spec=pltpu.PrefetchScalarGridSpec(
            num_scalar_prefetch=1,
            grid=(),
            in_specs=[vmem_spec] * (len(blocks) + 2 + len(arrived)) + [any_spec] * len(after),
            out_specs=vmem_spec,
            scratch_shapes=[pltpu.VMEM((count, depth), BF16)],
        ),
        compiler_params=pltpu.CompilerParams(vmem_limit_bytes=VMEM_LIMIT),
        cost_estimate=QUICK,
    )(part.reshape(1), *blocks, gate_weight, up_weight, *arrived, *after)


def down_kernel(parts, block_count, after_count, step_rows, scalar_ref, *refs):
    hidden_refs = refs[:parts]
    down_ref = refs[parts]
    block_refs = refs[parts + 1 : parts + 1 + block_count]
    own_ref, sent_ref, hidden = refs[parts + 1 + block_count + after_count :]
    part_width = hidden_refs[0].shape[1]
    width = down_ref.shape[2]
    for p, ref in enumerate(hidden_refs):
        start = pl.multiple_of(scalar_ref[2 + p] * part_width, part_width)
        hidden[:, pl.ds(start, part_width)] = ref[...]
    scale = jnp.concatenate(
        [scale_of(ref[:, width:], step_rows, scalar_ref[0], scalar_ref[1]) for ref in block_refs], axis=0
    )
    middle = scale.shape[0] // 2
    tile = 512 if width % 512 == 0 else 256
    for j in range(width // tile):
        here = slice(j * tile, (j + 1) * tile)
        total = jnp.dot(hidden[...], down_ref[0, :, here], preferred_element_type=F32) * scale
        own_ref[:, here] = total[:middle]
        sent_ref[:, here] = total[middle:].astype(BF16)


def down_rows(hidden_parts, down_weight, blocks, step_rows, wanted, part_ids, after):
    parts = len(hidden_parts)
    count, part_width = hidden_parts[0].shape
    width = down_weight.shape[2]
    any_spec = pl.BlockSpec(memory_space=pl.ANY)
    vmem_spec = pl.BlockSpec(memory_space=pltpu.VMEM)
    return pl.pallas_call(
        functools.partial(down_kernel, parts, len(blocks), len(after), step_rows),
        out_shape=(
            jax.ShapeDtypeStruct((count // 2, width), F32),
            jax.ShapeDtypeStruct((count // 2, width), BF16),
        ),
        grid_spec=pltpu.PrefetchScalarGridSpec(
            num_scalar_prefetch=1,
            grid=(),
            in_specs=[vmem_spec] * (parts + 1 + len(blocks)) + [any_spec] * len(after),
            out_specs=(vmem_spec, vmem_spec),
            scratch_shapes=[pltpu.VMEM((count, parts * part_width), BF16)],
        ),
        compiler_params=pltpu.CompilerParams(vmem_limit_bytes=VMEM_LIMIT),
        cost_estimate=QUICK,
    )(jnp.stack(wanted + part_ids), *hidden_parts, down_weight, *blocks, *after)


def base_kernel(one_ref, two_ref, route_one_ref, route_two_ref, gate_one_ref, gate_two_ref, out_ref):
    step_rows, width = one_ref.shape
    top = route_one_ref.shape[0]
    out_ref[:step_rows, :width] = one_ref[...]
    out_ref[step_rows:, :width] = two_ref[...]
    column = lax.broadcasted_iota(jnp.int32, (top, EXTRA), 1)
    choice = lax.broadcasted_iota(jnp.int32, (top, EXTRA), 0)

    def placed(value, start):
        where = (column == choice + start).astype(BF16)
        return lax.dot_general(
            value.astype(BF16), where, (((0,), (0,)), ((), ())), preferred_element_type=F32
        )

    for place, route_ref, gate_ref in ((0, route_one_ref, gate_one_ref), (1, route_two_ref, gate_two_ref)):
        rest = gate_ref[...]
        names = route_ref[...].astype(F32)
        total = None
        for piece in range(PIECES):
            part = rest.astype(BF16).astype(F32)
            rest = rest - part
            term = placed(part, piece * top) + placed(names, EXTRA // 2 + piece * top)
            total = term if total is None else total + term
        out_ref[place * step_rows : (place + 1) * step_rows, width:] = total.astype(BF16)


def base_rows(tokens_one, tokens_two, routes_one, routes_two, gates_one, gates_two):
    step_rows, width = tokens_one.shape
    return pl.pallas_call(
        base_kernel,
        out_shape=jax.ShapeDtypeStruct((2 * step_rows, width + EXTRA), BF16),
        in_specs=[pl.BlockSpec(memory_space=pltpu.VMEM)] * 6,
        out_specs=pl.BlockSpec(memory_space=pltpu.VMEM),
        compiler_params=pltpu.CompilerParams(vmem_limit_bytes=VMEM_LIMIT),
    )(tokens_one, tokens_two, routes_one.T, routes_two.T, gates_one.T, gates_two.T)


def shifted(value, axis, size, step):
    return lax.ppermute(value, axis, [(i, (i + step) % size) for i in range(size)])


def flipped(value, size, bits):
    return lax.ppermute(value, "ep", [(i, i ^ bits) for i in range(size)])


def shards(
    tokens_one,
    tokens_two,
    routes_one,
    routes_two,
    gates_one,
    gates_two,
    place_before,
    swap_flags,
    gate_weight,
    up_weight,
    down_weight,
):
    ep = lax.axis_size("ep")
    rep = lax.axis_size("rep")
    me = lax.axis_index("ep")
    y = lax.axis_index("rep")
    half = ep // 2
    z_count = ep // 4
    row_count, width = tokens_one.shape
    part_width = gate_weight.shape[2] // rep
    indices = jnp.arange(ep, dtype=jnp.int32)

    expert = jnp.sum(jnp.where(place_before == me, indices, 0))
    flag = jnp.sum(jnp.where(indices[:half] == me % half, swap_flags, 0))
    after = jnp.where(flag == 1, jnp.where(me < half, me + half, me - half), me)
    wanted = [expert, after]

    both = base_rows(tokens_one, tokens_two, routes_one, routes_two, gates_one, gates_two)
    part_ids = [y] + [(y - step) % rep for step in range(1, rep)]

    groups = min(4, z_count)
    per_group = z_count // groups
    members = [[group * per_group + i for i in range(per_group)] for group in (0, 2, 3, 1)[:groups]]
    along_z = [[both if r == 0 else flipped(both, ep, 4 * r) for r in group] for group in members]
    state = [dict() for _ in range(groups)]
    gate_weight, up_weight, down_weight = load([gate_weight, up_weight, down_weight], [both])
    last = []

    def gather(g):
        blocks = along_z[g] + [flipped(value, ep, 2) for value in along_z[g]]
        state[g]["blocks"] = blocks + [flipped(value, ep, 1) for value in blocks]

    def send_sums(g):
        state[g]["arrived"] = []
        for step in range(1, rep):
            partial = sums(
                state[g]["blocks"], gate_weight, up_weight, (y + step) % rep, part_width, [], last
            )
            last[:] = [partial]
            state[g]["arrived"].append(shifted(partial, "rep", rep, step))

    def send_hidden(g):
        hidden = sums(state[g]["blocks"], gate_weight, up_weight, y, part_width, state[g]["arrived"], last)
        last[:] = [hidden]
        state[g]["hidden"] = [hidden] + [shifted(hidden, "rep", rep, step) for step in range(1, rep)]

    def send_core(g):
        own, sent = down_rows(
            state[g]["hidden"], down_weight, state[g]["blocks"], row_count, wanted, part_ids, last
        )
        last[:] = [sent]
        state[g]["own"], state[g]["core"] = own, flipped(sent, ep, 1)

    def send_x(g):
        own, core = state[g]["own"], state[g]["core"]
        middle = own.shape[0] // 2
        far = (own[middle:] + core[middle:].astype(F32)).astype(BF16)
        last.append(far)
        state[g]["x"] = flipped(far, ep, 2)

    def send_z(g):
        own, core = state[g]["own"], state[g]["core"]
        middle = own.shape[0] // 2
        near = own[:middle] + core[:middle].astype(F32) + state[g]["x"].astype(F32)
        near = near.reshape(per_group, 2 * row_count, width)
        state[g]["z"] = []
        for place, r in enumerate(members[g]):
            if r == 0:
                state[g]["z"].append(near[place])
            else:
                block = near[place].astype(BF16)
                last.append(block)
                state[g]["z"].append(flipped(block, ep, 4 * r))

    stages = (gather, send_sums, send_hidden, send_core, send_x, send_z)
    for turn in range(groups + len(stages) - 1):
        for stage in reversed(range(len(stages))):
            if 0 <= turn - stage < groups:
                stages[stage](turn - stage)

    total = None
    for g in range(groups):
        for block in state[g]["z"]:
            total = block.astype(F32) if total is None else total + block.astype(F32)
    return total[:row_count].astype(BF16), total[row_count:].astype(BF16)


def solution(mesh):
    return jax.shard_map(
        shards,
        mesh=mesh,
        in_specs=(
            P("ep", "rep"),
            P("ep", "rep"),
            P("ep", None),
            P("ep", None),
            P("ep", None),
            P("ep", None),
            P(),
            P(),
            P("ep", "rep", None),
            P("ep", "rep", None),
            P("ep", None, "rep"),
        ),
        out_specs=(P("ep", "rep"), P("ep", "rep")),
        check_vma=False,
    )
```

```python
import functools
import math

import jax
import jax.numpy as jnp
from jax import lax
from jax.experimental import pallas as pl
from jax.experimental.pallas import tpu as pltpu
from jax.sharding import PartitionSpec as P

VMEM_LIMIT = 20 * 1024 * 1024
QUICK = pl.CostEstimate(flops=1, bytes_accessed=1, transcendentals=0)
F32 = jnp.float32
BF16 = jnp.bfloat16
EXTRA = 128
PIECES = 3


def scale_of(extra, step_rows, one, two):
    values = extra.astype(F32)
    names = pltpu.roll(values, EXTRA // 2, 1)
    row = lax.broadcasted_iota(jnp.int32, values.shape, 0)
    lane = lax.broadcasted_iota(jnp.int32, values.shape, 1)
    wanted = jnp.where(row % (2 * step_rows) < step_rows, one, two).astype(F32)
    chosen = jnp.logical_and(names == wanted, lane < EXTRA // 2)
    return jnp.sum(jnp.where(chosen, values, 0.0), axis=1, keepdims=True)


def in_hbm(array):
    return pltpu.with_memory_space_constraint(array, pltpu.HBM)


def in_vmem(array):
    return pltpu.with_memory_space_constraint(array, pltpu.VMEM)


def vmem_limit(*shapes):
    return sum(2 * math.prod(shape) for shape in shapes) + 5 * 1024 * 1024


def load_kernel(count, *refs):
    sems = refs[2 * count]
    copies = [pltpu.make_async_copy(refs[i], refs[count + i], sems.at[i]) for i in range(count)]
    for copy in copies:
        copy.start()
    for copy in copies:
        copy.wait()


def load(arrays, after):
    count = len(arrays)
    any_spec = pl.BlockSpec(memory_space=pl.ANY)
    return pl.pallas_call(
        lambda *refs: load_kernel(count, *refs[:count], *refs[count + len(after) :]),
        out_shape=[pltpu.VMEM(array.shape, array.dtype) for array in arrays],
        in_specs=[any_spec] * (count + len(after)),
        out_specs=[pl.BlockSpec(memory_space=pltpu.VMEM)] * count,
        scratch_shapes=[pltpu.SemaphoreType.DMA((count,))],
        compiler_params=pltpu.CompilerParams(vmem_limit_bytes=VMEM_LIMIT),
        cost_estimate=QUICK,
    )(*[in_hbm(array) for array in arrays], *after)


def sums_kernel(block_count, arrived_count, after_count, part_ref, *refs):
    block_refs = refs[:block_count]
    gate_ref, up_ref = refs[block_count : block_count + 2]
    arrived_refs = refs[block_count + 2 : block_count + 2 + arrived_count]
    out_ref, rows = refs[block_count + 2 + arrived_count + after_count :]
    depth = rows.shape[1]
    part_width = out_ref.shape[-1]
    tile = 256 if part_width % 256 == 0 else part_width
    start = 0
    for ref in block_refs:
        rows[start : start + ref.shape[0]] = ref[:, :depth]
        start += ref.shape[0]
    for j in range(part_width // tile):
        span = pl.ds(pl.multiple_of(part_ref[0] * part_width + j * tile, tile), tile)
        here = slice(j * tile, (j + 1) * tile)
        gate = jnp.dot(rows[...], gate_ref[0, :, span], preferred_element_type=F32)
        up = jnp.dot(rows[...], up_ref[0, :, span], preferred_element_type=F32)
        if arrived_count == 0:
            out_ref[0, :, here] = gate.astype(out_ref.dtype)
            out_ref[1, :, here] = up.astype(out_ref.dtype)
        else:
            for ref in arrived_refs:
                gate = gate + ref[0, :, here].astype(F32)
                up = up + ref[1, :, here].astype(F32)
            out_ref[:, here] = (gate / (1.0 + jnp.exp(-gate)) * up).astype(out_ref.dtype)


def sums(blocks, gate_weight, up_weight, part, part_width, arrived, after):
    count = sum(block.shape[0] for block in blocks)
    depth = gate_weight.shape[1]
    out_shape = (count, part_width) if arrived else (2, count, part_width)
    any_spec = pl.BlockSpec(memory_space=pl.ANY)
    vmem_spec = pl.BlockSpec(memory_space=pltpu.VMEM)
    return pl.pallas_call(
        functools.partial(sums_kernel, len(blocks), len(arrived), len(after)),
        out_shape=jax.ShapeDtypeStruct(out_shape, BF16),
        grid_spec=pltpu.PrefetchScalarGridSpec(
            num_scalar_prefetch=1,
            grid=(),
            in_specs=[vmem_spec] * (len(blocks) + 2 + len(arrived)) + [any_spec] * len(after),
            out_specs=vmem_spec,
            scratch_shapes=[pltpu.VMEM((count, depth), BF16)],
        ),
        compiler_params=pltpu.CompilerParams(
            vmem_limit_bytes=vmem_limit(
                (count, depth), *[block.shape for block in blocks], *[pair.shape for pair in arrived], out_shape
            )
        ),
        cost_estimate=QUICK,
    )(part.reshape(1), *blocks, in_vmem(gate_weight), in_vmem(up_weight), *arrived, *after)


def down_kernel(parts, block_count, after_count, step_rows, scalar_ref, *refs):
    hidden_refs = refs[:parts]
    down_ref = refs[parts]
    block_refs = refs[parts + 1 : parts + 1 + block_count]
    own_ref, sent_ref, hidden = refs[parts + 1 + block_count + after_count :]
    part_width = hidden_refs[0].shape[1]
    width = down_ref.shape[2]
    for p, ref in enumerate(hidden_refs):
        start = pl.multiple_of(scalar_ref[2 + p] * part_width, part_width)
        hidden[:, pl.ds(start, part_width)] = ref[...]
    scale = jnp.concatenate(
        [scale_of(ref[:, width:], step_rows, scalar_ref[0], scalar_ref[1]) for ref in block_refs], axis=0
    )
    middle = scale.shape[0] // 2
    tile = 512 if width % 512 == 0 else 256
    for j in range(width // tile):
        here = slice(j * tile, (j + 1) * tile)
        total = jnp.dot(hidden[...], down_ref[0, :, here], preferred_element_type=F32) * scale
        own_ref[:, here] = total[:middle]
        sent_ref[:, here] = total[middle:].astype(BF16)


def down_rows(hidden_parts, down_weight, blocks, step_rows, wanted, part_ids, after):
    parts = len(hidden_parts)
    count, part_width = hidden_parts[0].shape
    width = down_weight.shape[2]
    any_spec = pl.BlockSpec(memory_space=pl.ANY)
    vmem_spec = pl.BlockSpec(memory_space=pltpu.VMEM)
    return pl.pallas_call(
        functools.partial(down_kernel, parts, len(blocks), len(after), step_rows),
        out_shape=(
            jax.ShapeDtypeStruct((count // 2, width), F32),
            jax.ShapeDtypeStruct((count // 2, width), BF16),
        ),
        grid_spec=pltpu.PrefetchScalarGridSpec(
            num_scalar_prefetch=1,
            grid=(),
            in_specs=[vmem_spec] * (parts + 1 + len(blocks)) + [any_spec] * len(after),
            out_specs=(vmem_spec, vmem_spec),
            scratch_shapes=[pltpu.VMEM((count, parts * part_width), BF16)],
        ),
        compiler_params=pltpu.CompilerParams(
            vmem_limit_bytes=vmem_limit(
                (2 * count, parts * part_width), *[block.shape for block in blocks], (3 * count // 2, width)
            )
        ),
        cost_estimate=QUICK,
    )(jnp.stack(wanted + part_ids), *hidden_parts, in_vmem(down_weight), *blocks, *after)


def base_kernel(one_ref, two_ref, route_one_ref, route_two_ref, gate_one_ref, gate_two_ref, out_ref):
    step_rows, width = one_ref.shape
    top = route_one_ref.shape[0]
    out_ref[:step_rows, :width] = one_ref[...]
    out_ref[step_rows:, :width] = two_ref[...]
    column = lax.broadcasted_iota(jnp.int32, (top, EXTRA), 1)
    choice = lax.broadcasted_iota(jnp.int32, (top, EXTRA), 0)

    def placed(value, start):
        where = (column == choice + start).astype(BF16)
        return lax.dot_general(
            value.astype(BF16), where, (((0,), (0,)), ((), ())), preferred_element_type=F32
        )

    for place, route_ref, gate_ref in ((0, route_one_ref, gate_one_ref), (1, route_two_ref, gate_two_ref)):
        rest = gate_ref[...]
        names = route_ref[...].astype(F32)
        total = None
        for piece in range(PIECES):
            part = rest.astype(BF16).astype(F32)
            rest = rest - part
            term = placed(part, piece * top) + placed(names, EXTRA // 2 + piece * top)
            total = term if total is None else total + term
        out_ref[place * step_rows : (place + 1) * step_rows, width:] = total.astype(BF16)


def base_rows(tokens_one, tokens_two, routes_one, routes_two, gates_one, gates_two):
    step_rows, width = tokens_one.shape
    return pl.pallas_call(
        base_kernel,
        out_shape=jax.ShapeDtypeStruct((2 * step_rows, width + EXTRA), BF16),
        in_specs=[pl.BlockSpec(memory_space=pltpu.VMEM)] * 6,
        out_specs=pl.BlockSpec(memory_space=pltpu.VMEM),
        compiler_params=pltpu.CompilerParams(vmem_limit_bytes=VMEM_LIMIT),
    )(*[in_hbm(array) for array in (tokens_one, tokens_two, routes_one.T, routes_two.T, gates_one.T, gates_two.T)])


def shifted(value, axis, size, step):
    return lax.ppermute(value, axis, [(i, (i + step) % size) for i in range(size)])


def flipped(value, size, bits):
    return lax.ppermute(value, "ep", [(i, i ^ bits) for i in range(size)])


def shards(
    tokens_one,
    tokens_two,
    routes_one,
    routes_two,
    gates_one,
    gates_two,
    place_before,
    swap_flags,
    gate_weight,
    up_weight,
    down_weight,
):
    ep = lax.axis_size("ep")
    rep = lax.axis_size("rep")
    me = lax.axis_index("ep")
    y = lax.axis_index("rep")
    half = ep // 2
    z_count = ep // 4
    row_count, width = tokens_one.shape
    part_width = gate_weight.shape[2] // rep
    indices = jnp.arange(ep, dtype=jnp.int32)

    expert = jnp.sum(jnp.where(place_before == me, indices, 0))
    flag = jnp.sum(jnp.where(indices[:half] == me % half, swap_flags, 0))
    after = jnp.where(flag == 1, jnp.where(me < half, me + half, me - half), me)
    wanted = [expert, after]

    both = base_rows(tokens_one, tokens_two, routes_one, routes_two, gates_one, gates_two)
    part_ids = [y] + [(y - step) % rep for step in range(1, rep)]

    groups = 4
    per_group = z_count // groups
    members = [[group * per_group + i for i in range(per_group)] for group in (0, 2, 3, 1)]
    columns = [[z * 4 + k for z in range(z_count)] for k in range(4)]
    gathered = lax.all_gather(both, "ep", axis_index_groups=columns)
    place = me // 4
    along_z = [
        [both if r == 0 else lax.dynamic_index_in_dim(gathered, place ^ r, 0, keepdims=False) for r in group]
        for group in members
    ]
    gate_weight, up_weight = load([gate_weight, up_weight], [both])
    (down_weight,) = load([down_weight], [both, gate_weight])
    state = [dict() for _ in range(groups)]
    last = [down_weight]

    def follow(*values):
        held = lax.optimization_barrier(tuple(values) + tuple(last))
        return held[: len(values)]

    def ask_x(g):
        near = along_z[g] if g == 0 else follow(*along_z[g])
        state[g]["near"] = list(near)
        state[g]["across"] = [flipped(value, ep, 2) for value in near]

    def ask_core(g):
        across = list(follow(*state[g]["across"]))
        here = jnp.concatenate(state[g]["near"] + across, axis=0)
        state[g]["blocks"] = state[g]["near"] + across + [flipped(here, ep, 1)]

    def send_sums(g):
        state[g]["arrived"] = []
        for step in range(1, rep):
            partial = sums(
                state[g]["blocks"], gate_weight, up_weight, (y + step) % rep, part_width, [], last
            )
            last[:] = [partial]
            state[g]["arrived"].append(shifted(partial, "rep", rep, step))

    def send_hidden(g):
        hidden = sums(state[g]["blocks"], gate_weight, up_weight, y, part_width, state[g]["arrived"], last)
        last[:] = [hidden]
        state[g]["hidden"] = [hidden] + [shifted(hidden, "rep", rep, step) for step in range(1, rep)]

    def send_core(g):
        own, sent = down_rows(
            state[g]["hidden"], down_weight, state[g]["blocks"], row_count, wanted, part_ids, last
        )
        last[:] = [sent]
        state[g]["own"], state[g]["core"] = own, flipped(sent, ep, 1)

    def send_x(g):
        own, core = state[g]["own"], state[g]["core"]
        middle = own.shape[0] // 2
        (core,) = follow(core)
        far = (own[middle:] + core[middle:].astype(F32)).astype(BF16)
        last.append(far)
        state[g]["x"] = flipped(far, ep, 2)

    def send_z(g):
        own, core = state[g]["own"], state[g]["core"]
        middle = own.shape[0] // 2
        (across,) = follow(state[g]["x"])
        near = own[:middle] + core[:middle].astype(F32) + across.astype(F32)
        near = near.reshape(per_group, 2 * row_count, width)
        state[g]["z"] = []
        for place, r in enumerate(members[g]):
            if r == 0:
                last.append(near[place])
                state[g]["z"].append(near[place])
            else:
                block = near[place].astype(BF16)
                last.append(block)
                state[g]["z"].append(flipped(block, ep, 4 * r))

    totals = []

    def finish(g):
        total = totals[-1] if totals else None
        for block in state[g]["z"]:
            total = block.astype(F32) if total is None else total + block.astype(F32)
        totals.append(total)
        last.append(total)

    def run(*turns):
        for stage, g in turns:
            stage(g)

    run((ask_x, 0), (ask_core, 0), (send_sums, 0), (ask_x, 1), (send_hidden, 0), (ask_core, 1), (ask_x, 2))
    run((send_sums, 1), (send_core, 0), (send_x, 0), (send_hidden, 1), (ask_x, 3), (ask_core, 2), (send_sums, 2))
    run((send_core, 1), (send_z, 0), (finish, 0), (send_x, 1), (ask_core, 3), (send_sums, 3), (send_hidden, 2))
    run((send_z, 1), (send_core, 2), (send_hidden, 3), (send_x, 2), (finish, 1), (send_core, 3), (send_x, 3))
    run((send_z, 2), (send_z, 3), (finish, 2), (finish, 3))
    total = totals[-1]
    return total[:row_count].astype(BF16), total[row_count:].astype(BF16)


def solution(mesh):
    return jax.shard_map(
        shards,
        mesh=mesh,
        in_specs=(
            P("ep", "rep"),
            P("ep", "rep"),
            P("ep", None),
            P("ep", None),
            P("ep", None),
            P("ep", None),
            P(),
            P(),
            P("ep", "rep", None),
            P("ep", "rep", None),
            P("ep", None, "rep"),
        ),
        out_specs=(P("ep", "rep"), P("ep", "rep")),
        check_vma=False,
    )
```

```python
import functools
import math

import jax
import jax.numpy as jnp
from jax import lax
from jax.experimental import pallas as pl
from jax.experimental.pallas import tpu as pltpu
from jax.sharding import PartitionSpec as P

VMEM_LIMIT = 8 * 1024 * 1024
QUICK = pl.CostEstimate(flops=1, bytes_accessed=1, transcendentals=0)
F32 = jnp.float32
BF16 = jnp.bfloat16
EXTRA = 128
PIECES = 3


def scale_of(extra, step_rows, one, two):
    values = extra.astype(F32)
    names = pltpu.roll(values, EXTRA // 2, 1)
    row = lax.broadcasted_iota(jnp.int32, values.shape, 0)
    lane = lax.broadcasted_iota(jnp.int32, values.shape, 1)
    wanted = jnp.where(row % (2 * step_rows) < step_rows, one, two).astype(F32)
    chosen = jnp.logical_and(names == wanted, lane < EXTRA // 2)
    return jnp.sum(jnp.where(chosen, values, 0.0), axis=1, keepdims=True)


def in_hbm(array):
    return pltpu.with_memory_space_constraint(array, pltpu.HBM)


def in_vmem(array):
    return pltpu.with_memory_space_constraint(array, pltpu.VMEM)


def vmem_limit(*shapes):
    return sum(2 * math.prod(shape) for shape in shapes) + 5 * 1024 * 1024


def load_kernel(count, *refs):
    sems = refs[2 * count]
    copies = [pltpu.make_async_copy(refs[i], refs[count + i], sems.at[i]) for i in range(count)]
    for copy in copies:
        copy.start()
    for copy in copies:
        copy.wait()


def load(arrays, after):
    count = len(arrays)
    any_spec = pl.BlockSpec(memory_space=pl.ANY)
    return pl.pallas_call(
        lambda *refs: load_kernel(count, *refs[:count], *refs[count + len(after) :]),
        out_shape=[pltpu.VMEM(array.shape, array.dtype) for array in arrays],
        in_specs=[any_spec] * (count + len(after)),
        out_specs=[pl.BlockSpec(memory_space=pltpu.VMEM)] * count,
        scratch_shapes=[pltpu.SemaphoreType.DMA((count,))],
        compiler_params=pltpu.CompilerParams(vmem_limit_bytes=VMEM_LIMIT),
        cost_estimate=QUICK,
    )(*[in_hbm(array) for array in arrays], *after)


def sums_kernel(block_count, arrived_count, after_count, part, scalar_ref, *refs):
    block_refs = refs[:block_count]
    gate_ref, up_ref = refs[block_count : block_count + 2]
    arrived_refs = refs[block_count + 2 : block_count + 2 + arrived_count]
    out_refs = refs[block_count + 2 + arrived_count + after_count : -1]
    rows = refs[-1]
    depth = rows.shape[1]
    part_width = out_refs[0].shape[1]
    tile = 256 if part_width % 256 == 0 else part_width
    start = 0
    for ref in block_refs:
        rows[start : start + ref.shape[0]] = ref[:, :depth]
        start += ref.shape[0]
    for j in range(part_width // tile):
        span = pl.ds(pl.multiple_of(scalar_ref[part] * part_width + j * tile, tile), tile)
        here = slice(j * tile, (j + 1) * tile)
        gate = jnp.dot(rows[...], gate_ref[0, :, span], preferred_element_type=F32)
        up = jnp.dot(rows[...], up_ref[0, :, span], preferred_element_type=F32)
        if arrived_count == 0:
            out_refs[0][:, here] = gate.astype(BF16)
            out_refs[1][:, here] = up.astype(BF16)
        else:
            for gate_in, up_in in zip(arrived_refs[::2], arrived_refs[1::2]):
                gate = gate + gate_in[:, here].astype(F32)
                up = up + up_in[:, here].astype(F32)
            out_refs[0][:, here] = (gate / (1.0 + jnp.exp(-gate)) * up).astype(BF16)


def sums(blocks, gate_weight, up_weight, scalars, part, part_width, arrived, after):
    count = sum(block.shape[0] for block in blocks)
    depth = gate_weight.shape[1]
    outs = 1 if arrived else 2
    out_shape = (count, part_width)
    any_spec = pl.BlockSpec(memory_space=pl.ANY)
    vmem_spec = pl.BlockSpec(memory_space=pltpu.VMEM)
    return pl.pallas_call(
        functools.partial(sums_kernel, len(blocks), len(arrived), len(after), part),
        out_shape=[jax.ShapeDtypeStruct(out_shape, BF16)] * outs,
        grid_spec=pltpu.PrefetchScalarGridSpec(
            num_scalar_prefetch=1,
            grid=(),
            in_specs=[vmem_spec] * (len(blocks) + 2 + len(arrived)) + [any_spec] * len(after),
            out_specs=[vmem_spec] * outs,
            scratch_shapes=[pltpu.VMEM((count, depth), BF16)],
        ),
        compiler_params=pltpu.CompilerParams(
            vmem_limit_bytes=vmem_limit(
                (count, depth), *[block.shape for block in blocks], *[pair.shape for pair in arrived], *[out_shape] * outs
            )
        ),
        cost_estimate=QUICK,
    )(scalars, *blocks, in_vmem(gate_weight), in_vmem(up_weight), *arrived, *after)


def down_kernel(parts, block_count, after_count, step_rows, scalar_ref, *refs):
    hidden_refs = refs[:parts]
    down_ref = refs[parts]
    block_refs = refs[parts + 1 : parts + 1 + block_count]
    near_ref, far_ref, sent_near_ref, sent_far_ref, hidden = refs[parts + 1 + block_count + after_count :]
    part_width = hidden_refs[0].shape[1]
    width = down_ref.shape[2]
    for p, ref in enumerate(hidden_refs):
        start = pl.multiple_of(scalar_ref[2 + p] * part_width, part_width)
        hidden[:, pl.ds(start, part_width)] = ref[...]
    scale = jnp.concatenate(
        [scale_of(ref[:, width:], step_rows, scalar_ref[0], scalar_ref[1]) for ref in block_refs], axis=0
    )
    quarter = scale.shape[0] // 4
    tile = 512 if width % 512 == 0 else 256
    for j in range(width // tile):
        here = slice(j * tile, (j + 1) * tile)
        total = jnp.dot(hidden[...], down_ref[0, :, here], preferred_element_type=F32) * scale
        for i, ref in enumerate((near_ref, far_ref, sent_near_ref, sent_far_ref)):
            ref[:, here] = total[i * quarter : (i + 1) * quarter].astype(ref.dtype)


def down_rows(hidden_parts, down_weight, blocks, step_rows, scalars, after):
    parts = len(hidden_parts)
    count, part_width = hidden_parts[0].shape
    width = down_weight.shape[2]
    any_spec = pl.BlockSpec(memory_space=pl.ANY)
    vmem_spec = pl.BlockSpec(memory_space=pltpu.VMEM)
    return pl.pallas_call(
        functools.partial(down_kernel, parts, len(blocks), len(after), step_rows),
        out_shape=[jax.ShapeDtypeStruct((count // 4, width), dtype) for dtype in (F32, F32, BF16, BF16)],
        grid_spec=pltpu.PrefetchScalarGridSpec(
            num_scalar_prefetch=1,
            grid=(),
            in_specs=[vmem_spec] * (parts + 1 + len(blocks)) + [any_spec] * len(after),
            out_specs=[vmem_spec] * 4,
            scratch_shapes=[pltpu.VMEM((count, parts * part_width), BF16)],
        ),
        compiler_params=pltpu.CompilerParams(
            vmem_limit_bytes=vmem_limit(
                (2 * count, parts * part_width), *[block.shape for block in blocks], (3 * count // 2, width)
            )
        ),
        cost_estimate=QUICK,
    )(scalars, *hidden_parts, in_vmem(down_weight), *blocks, *after)


def base_kernel(one_ref, two_ref, route_one_ref, route_two_ref, gate_one_ref, gate_two_ref, out_ref):
    step_rows, width = one_ref.shape
    top = route_one_ref.shape[0]
    out_ref[:step_rows, :width] = one_ref[...]
    out_ref[step_rows:, :width] = two_ref[...]
    column = lax.broadcasted_iota(jnp.int32, (top, EXTRA), 1)
    choice = lax.broadcasted_iota(jnp.int32, (top, EXTRA), 0)

    def placed(value, start):
        where = (column == choice + start).astype(BF16)
        return lax.dot_general(
            value.astype(BF16), where, (((0,), (0,)), ((), ())), preferred_element_type=F32
        )

    for place, route_ref, gate_ref in ((0, route_one_ref, gate_one_ref), (1, route_two_ref, gate_two_ref)):
        rest = gate_ref[...]
        names = route_ref[...].astype(F32)
        total = None
        for piece in range(PIECES):
            part = rest.astype(BF16).astype(F32)
            rest = rest - part
            term = placed(part, piece * top) + placed(names, EXTRA // 2 + piece * top)
            total = term if total is None else total + term
        out_ref[place * step_rows : (place + 1) * step_rows, width:] = total.astype(BF16)


def base_rows(tokens_one, tokens_two, routes_one, routes_two, gates_one, gates_two):
    step_rows, width = tokens_one.shape
    return pl.pallas_call(
        base_kernel,
        out_shape=jax.ShapeDtypeStruct((2 * step_rows, width + EXTRA), BF16),
        in_specs=[pl.BlockSpec(memory_space=pltpu.VMEM)] * 6,
        out_specs=pl.BlockSpec(memory_space=pltpu.VMEM),
        compiler_params=pltpu.CompilerParams(vmem_limit_bytes=VMEM_LIMIT),
    )(*[in_hbm(array) for array in (tokens_one, tokens_two, routes_one.T, routes_two.T, gates_one.T, gates_two.T)])


def shifted(value, axis, size, step):
    return lax.ppermute(value, axis, [(i, (i + step) % size) for i in range(size)])


def flipped(value, size, bits):
    return lax.ppermute(value, "ep", [(i, i ^ bits) for i in range(size)])


def shards(
    tokens_one,
    tokens_two,
    routes_one,
    routes_two,
    gates_one,
    gates_two,
    place_before,
    swap_flags,
    gate_weight,
    up_weight,
    down_weight,
):
    ep = lax.axis_size("ep")
    rep = lax.axis_size("rep")
    me = lax.axis_index("ep")
    y = lax.axis_index("rep")
    half = ep // 2
    z_count = ep // 4
    row_count, width = tokens_one.shape
    part_width = gate_weight.shape[2] // rep
    indices = jnp.arange(ep, dtype=jnp.int32)

    part_ids = [y] + [(y - step) % rep for step in range(1, rep)]
    turn_ids = [(y + step) % rep for step in range(1, rep)]
    expert = jnp.sum(jnp.where(place_before == me, indices, 0))
    flag = jnp.sum(jnp.where(indices[:half] == me % half, swap_flags, 0))
    after = jnp.where(flag == 1, jnp.where(me < half, me + half, me - half), me)
    scalars = jnp.stack([expert, after] + part_ids + turn_ids).astype(jnp.int32)

    both = base_rows(tokens_one, tokens_two, routes_one, routes_two, gates_one, gates_two)

    groups = 4
    per_group = z_count // groups
    members = [[group * per_group + i for i in range(per_group)] for group in (0, 2, 3, 1)]
    along_z = [[both if r == 0 else flipped(both, ep, 4 * r) for r in group] for group in members]
    gate_weight, up_weight = load([gate_weight, up_weight], [both, scalars])
    (down_weight,) = load([down_weight], [gate_weight])
    state = [dict() for _ in range(groups)]
    last = [down_weight]

    def follow(*values):
        held = lax.optimization_barrier(tuple(values) + tuple(last))
        return held[: len(values)]

    def ask_x(g):
        near = along_z[g] if g == 0 else follow(*along_z[g])
        state[g]["near"] = list(near)
        state[g]["across"] = [flipped(value, ep, 2) for value in near]

    def ask_core(g):
        across = list(follow(*state[g]["across"]))
        here = state[g]["near"] + across
        state[g]["blocks"] = here + [flipped(value, ep, 1) for value in here]

    def hold_z(g):
        last.extend(along_z[g])

    def hold_x(g):
        last.extend(state[g]["across"])

    def send_sums(g):
        state[g]["arrived"] = []
        for step in range(1, rep):
            partial = sums(
                state[g]["blocks"], gate_weight, up_weight, scalars, 1 + rep + step, part_width, [], last
            )
            last[:] = [partial[1]]
            state[g]["arrived"] += [shifted(value, "rep", rep, step) for value in partial]

    def send_hidden(g):
        (hidden,) = sums(
            state[g]["blocks"], gate_weight, up_weight, scalars, 2, part_width, state[g]["arrived"], last
        )
        last[:] = [hidden]
        state[g]["hidden"] = [hidden] + [shifted(hidden, "rep", rep, step) for step in range(1, rep)]

    def send_core(g):
        near, far, sent_near, sent_far = down_rows(
            state[g]["hidden"], down_weight, state[g]["blocks"], row_count, scalars, last
        )
        last[:] = [sent_far]
        state[g]["own"] = near, far
        state[g]["core_far"] = flipped(sent_far, ep, 1)
        state[g]["core_near"] = flipped(sent_near, ep, 1)

    def send_x(g):
        (core,) = follow(state[g]["core_far"])
        far = (state[g]["own"][1] + core.astype(F32)).astype(BF16)
        last.append(far)
        state[g]["x"] = flipped(far, ep, 2)

    def send_z(g):
        core, across = follow(state[g]["core_near"], state[g]["x"])
        near = state[g]["own"][0] + core.astype(F32) + across.astype(F32)
        near = near.reshape(per_group, 2 * row_count, width)
        state[g]["z"] = []
        for place, r in enumerate(members[g]):
            if r == 0:
                last.append(near[place])
                state[g]["z"].append(near[place])
            else:
                block = near[place].astype(BF16)
                last.append(block)
                state[g]["z"].append(flipped(block, ep, 4 * r))

    totals = []

    def finish(g):
        total = totals[-1] if totals else None
        for block in state[g]["z"]:
            total = block.astype(F32) if total is None else total + block.astype(F32)
        totals.append(total)
        last.append(total)

    def run(*turns):
        for stage, g in turns:
            stage(g)

    run((ask_x, 0), (ask_core, 0), (hold_z, 1), (send_sums, 0), (ask_x, 1), (hold_x, 1), (send_hidden, 0), (ask_core, 1))
    run((hold_z, 2), (send_sums, 1), (ask_x, 2), (send_core, 0), (send_x, 0), (hold_x, 2), (send_hidden, 1))
    run((ask_core, 2), (hold_z, 3), (send_sums, 2), (ask_x, 3), (send_core, 1), (send_z, 0), (finish, 0))
    run((send_x, 1), (hold_x, 3), (ask_core, 3), (send_hidden, 2), (send_sums, 3), (send_z, 1), (send_core, 2))
    run((send_hidden, 3), (send_x, 2), (finish, 1), (send_core, 3), (send_x, 3))
    run((send_z, 2), (send_z, 3), (finish, 2), (finish, 3))
    total = totals[-1]
    return total[:row_count].astype(BF16), total[row_count:].astype(BF16)


def solution(mesh):
    return jax.shard_map(
        shards,
        mesh=mesh,
        in_specs=(
            P("ep", "rep"),
            P("ep", "rep"),
            P("ep", None),
            P("ep", None),
            P("ep", None),
            P("ep", None),
            P(),
            P(),
            P("ep", "rep", None),
            P("ep", "rep", None),
            P("ep", None, "rep"),
        ),
        out_specs=(P("ep", "rep"), P("ep", "rep")),
        check_vma=False,
    )
```

```python
import functools
import math

import jax
import jax.numpy as jnp
from jax import lax
from jax.experimental import pallas as pl
from jax.experimental.pallas import tpu as pltpu
from jax.sharding import PartitionSpec as P

VMEM_LIMIT = 8 * 1024 * 1024
QUICK = pl.CostEstimate(flops=1, bytes_accessed=1, transcendentals=0)
F32 = jnp.float32
BF16 = jnp.bfloat16
EXTRA = 128
PIECES = 3


def scale_of(extra, step_rows, one, two):
    values = extra.astype(F32)
    names = pltpu.roll(values, EXTRA // 2, 1)
    row = lax.broadcasted_iota(jnp.int32, values.shape, 0)
    lane = lax.broadcasted_iota(jnp.int32, values.shape, 1)
    wanted = jnp.where(row % (2 * step_rows) < step_rows, one, two).astype(F32)
    chosen = jnp.logical_and(names == wanted, lane < EXTRA // 2)
    return jnp.sum(jnp.where(chosen, values, 0.0), axis=1, keepdims=True)


def in_hbm(array):
    return pltpu.with_memory_space_constraint(array, pltpu.HBM)


def in_vmem(array):
    return pltpu.with_memory_space_constraint(array, pltpu.VMEM)


def vmem_limit(*shapes):
    return sum(2 * math.prod(shape) for shape in shapes) + 5 * 1024 * 1024


def load_kernel(count, *refs):
    sems = refs[2 * count]
    copies = [pltpu.make_async_copy(refs[i], refs[count + i], sems.at[i]) for i in range(count)]
    for copy in copies:
        copy.start()
    for copy in copies:
        copy.wait()


def load(arrays, after):
    count = len(arrays)
    any_spec = pl.BlockSpec(memory_space=pl.ANY)
    return pl.pallas_call(
        lambda *refs: load_kernel(count, *refs[:count], *refs[count + len(after) :]),
        out_shape=[pltpu.VMEM(array.shape, array.dtype) for array in arrays],
        in_specs=[any_spec] * (count + len(after)),
        out_specs=[pl.BlockSpec(memory_space=pltpu.VMEM)] * count,
        scratch_shapes=[pltpu.SemaphoreType.DMA((count,))],
        compiler_params=pltpu.CompilerParams(vmem_limit_bytes=VMEM_LIMIT),
        cost_estimate=QUICK,
    )(*[in_hbm(array) for array in arrays], *after)


def sums_kernel(block_count, arrived_count, after_count, part, scalar_ref, *refs):
    block_refs = refs[:block_count]
    gate_ref, up_ref = refs[block_count : block_count + 2]
    arrived_refs = refs[block_count + 2 : block_count + 2 + arrived_count]
    out_ref, rows = refs[block_count + 2 + arrived_count + after_count :]
    depth = rows.shape[1]
    part_width = out_ref.shape[-1]
    tile = 256 if part_width % 256 == 0 else part_width
    start = 0
    for ref in block_refs:
        rows[start : start + ref.shape[0]] = ref[:, :depth]
        start += ref.shape[0]
    for j in range(part_width // tile):
        span = pl.ds(pl.multiple_of(scalar_ref[part] * part_width + j * tile, tile), tile)
        here = slice(j * tile, (j + 1) * tile)
        gate = jnp.dot(rows[...], gate_ref[0, :, span], preferred_element_type=F32)
        up = jnp.dot(rows[...], up_ref[0, :, span], preferred_element_type=F32)
        if arrived_count == 0:
            out_ref[0, :, here] = gate.astype(BF16)
            out_ref[1, :, here] = up.astype(BF16)
        else:
            for ref in arrived_refs:
                gate = gate + ref[0, :, here].astype(F32)
                up = up + ref[1, :, here].astype(F32)
            out_ref[:, here] = (gate / (1.0 + jnp.exp(-gate)) * up).astype(BF16)


def sums(blocks, gate_weight, up_weight, scalars, part, part_width, arrived, after):
    count = sum(block.shape[0] for block in blocks)
    depth = gate_weight.shape[1]
    out_shape = (count, part_width) if arrived else (2, count, part_width)
    any_spec = pl.BlockSpec(memory_space=pl.ANY)
    vmem_spec = pl.BlockSpec(memory_space=pltpu.VMEM)
    return pl.pallas_call(
        functools.partial(sums_kernel, len(blocks), len(arrived), len(after), part),
        out_shape=jax.ShapeDtypeStruct(out_shape, BF16),
        grid_spec=pltpu.PrefetchScalarGridSpec(
            num_scalar_prefetch=1,
            grid=(),
            in_specs=[vmem_spec] * (len(blocks) + 2 + len(arrived)) + [any_spec] * len(after),
            out_specs=vmem_spec,
            scratch_shapes=[pltpu.VMEM((count, depth), BF16)],
        ),
        compiler_params=pltpu.CompilerParams(
            vmem_limit_bytes=vmem_limit(
                (count, depth), *[block.shape for block in blocks], *[pair.shape for pair in arrived], out_shape
            )
        ),
        cost_estimate=QUICK,
    )(scalars, *blocks, in_vmem(gate_weight), in_vmem(up_weight), *arrived, *after)


def down_kernel(parts, block_count, after_count, step_rows, scalar_ref, *refs):
    hidden_refs = refs[:parts]
    down_ref = refs[parts]
    block_refs = refs[parts + 1 : parts + 1 + block_count]
    near_ref, far_ref, sent_near_ref, sent_far_ref, hidden = refs[parts + 1 + block_count + after_count :]
    part_width = hidden_refs[0].shape[1]
    width = down_ref.shape[2]
    for p, ref in enumerate(hidden_refs):
        start = pl.multiple_of(scalar_ref[2 + p] * part_width, part_width)
        hidden[:, pl.ds(start, part_width)] = ref[...]
    scale = jnp.concatenate(
        [scale_of(ref[:, width:], step_rows, scalar_ref[0], scalar_ref[1]) for ref in block_refs], axis=0
    )
    quarter = scale.shape[0] // 4
    tile = 512 if width % 512 == 0 else 256
    for j in range(width // tile):
        here = slice(j * tile, (j + 1) * tile)
        total = jnp.dot(hidden[...], down_ref[0, :, here], preferred_element_type=F32) * scale
        for i, ref in enumerate((near_ref, far_ref, sent_near_ref, sent_far_ref)):
            ref[:, here] = total[i * quarter : (i + 1) * quarter].astype(ref.dtype)


def down_rows(hidden_parts, down_weight, blocks, step_rows, scalars, after):
    parts = len(hidden_parts)
    count, part_width = hidden_parts[0].shape
    width = down_weight.shape[2]
    any_spec = pl.BlockSpec(memory_space=pl.ANY)
    vmem_spec = pl.BlockSpec(memory_space=pltpu.VMEM)
    return pl.pallas_call(
        functools.partial(down_kernel, parts, len(blocks), len(after), step_rows),
        out_shape=[jax.ShapeDtypeStruct((count // 4, width), dtype) for dtype in (F32, F32, BF16, BF16)],
        grid_spec=pltpu.PrefetchScalarGridSpec(
            num_scalar_prefetch=1,
            grid=(),
            in_specs=[vmem_spec] * (parts + 1 + len(blocks)) + [any_spec] * len(after),
            out_specs=[vmem_spec] * 4,
            scratch_shapes=[pltpu.VMEM((count, parts * part_width), BF16)],
        ),
        compiler_params=pltpu.CompilerParams(
            vmem_limit_bytes=vmem_limit(
                (2 * count, parts * part_width), *[block.shape for block in blocks], (3 * count // 2, width)
            )
        ),
        cost_estimate=QUICK,
    )(scalars, *hidden_parts, in_vmem(down_weight), *blocks, *after)


def base_kernel(one_ref, two_ref, route_one_ref, route_two_ref, gate_one_ref, gate_two_ref, out_ref):
    step_rows, width = one_ref.shape
    top = route_one_ref.shape[0]
    out_ref[:step_rows, :width] = one_ref[...]
    out_ref[step_rows:, :width] = two_ref[...]
    column = lax.broadcasted_iota(jnp.int32, (top, EXTRA), 1)
    choice = lax.broadcasted_iota(jnp.int32, (top, EXTRA), 0)

    def placed(value, start):
        where = (column == choice + start).astype(BF16)
        return lax.dot_general(
            value.astype(BF16), where, (((0,), (0,)), ((), ())), preferred_element_type=F32
        )

    for place, route_ref, gate_ref in ((0, route_one_ref, gate_one_ref), (1, route_two_ref, gate_two_ref)):
        rest = gate_ref[...]
        names = route_ref[...].astype(F32)
        total = None
        for piece in range(PIECES):
            part = rest.astype(BF16).astype(F32)
            rest = rest - part
            term = placed(part, piece * top) + placed(names, EXTRA // 2 + piece * top)
            total = term if total is None else total + term
        out_ref[place * step_rows : (place + 1) * step_rows, width:] = total.astype(BF16)


def base_rows(tokens_one, tokens_two, routes_one, routes_two, gates_one, gates_two):
    step_rows, width = tokens_one.shape
    return pl.pallas_call(
        base_kernel,
        out_shape=jax.ShapeDtypeStruct((2 * step_rows, width + EXTRA), BF16),
        in_specs=[pl.BlockSpec(memory_space=pltpu.VMEM)] * 6,
        out_specs=pl.BlockSpec(memory_space=pltpu.VMEM),
        compiler_params=pltpu.CompilerParams(vmem_limit_bytes=VMEM_LIMIT),
    )(*[in_hbm(array) for array in (tokens_one, tokens_two, routes_one.T, routes_two.T, gates_one.T, gates_two.T)])


def shifted(value, axis, size, step):
    return lax.ppermute(value, axis, [(i, (i + step) % size) for i in range(size)])


def flipped(value, size, bits):
    return lax.ppermute(value, "ep", [(i, i ^ bits) for i in range(size)])


def shards(
    tokens_one,
    tokens_two,
    routes_one,
    routes_two,
    gates_one,
    gates_two,
    place_before,
    swap_flags,
    gate_weight,
    up_weight,
    down_weight,
):
    ep = lax.axis_size("ep")
    rep = lax.axis_size("rep")
    me = lax.axis_index("ep")
    y = lax.axis_index("rep")
    half = ep // 2
    z_count = ep // 4
    row_count, width = tokens_one.shape
    part_width = gate_weight.shape[2] // rep
    indices = jnp.arange(ep, dtype=jnp.int32)

    part_ids = [y] + [(y - step) % rep for step in range(1, rep)]
    turn_ids = [(y + step) % rep for step in range(1, rep)]
    expert = jnp.sum(jnp.where(place_before == me, indices, 0))
    flag = jnp.sum(jnp.where(indices[:half] == me % half, swap_flags, 0))
    after = jnp.where(flag == 1, jnp.where(me < half, me + half, me - half), me)
    scalars = jnp.stack([expert, after] + part_ids + turn_ids).astype(jnp.int32)

    both = base_rows(tokens_one, tokens_two, routes_one, routes_two, gates_one, gates_two)

    groups = 4
    per_group = z_count // groups
    members = [[group * per_group + i for i in range(per_group)] for group in (0, 2, 3, 1)]
    along_z = [[both if r == 0 else flipped(both, ep, 4 * r) for r in group] for group in members]
    gate_weight, up_weight = load([gate_weight, up_weight], [both, scalars])
    (down_weight,) = load([down_weight], [gate_weight])
    state = [dict() for _ in range(groups)]
    last = [down_weight]

    def follow(*values):
        held = lax.optimization_barrier(tuple(values) + tuple(last))
        return held[: len(values)]

    def ask_x(g):
        near = along_z[g] if g == 0 else follow(*along_z[g])
        state[g]["near"] = list(near)
        state[g]["across"] = [flipped(value, ep, 2) for value in near]

    def ask_core(g):
        across = list(follow(*state[g]["across"]))
        here = state[g]["near"] + across
        state[g]["blocks"] = here + [flipped(value, ep, 1) for value in here]

    def hold_z(g):
        last.extend(along_z[g])

    def hold_x(g):
        last.extend(state[g]["across"])

    def send_sums(g):
        state[g]["arrived"] = []
        for step in range(1, rep):
            partial = sums(
                state[g]["blocks"], gate_weight, up_weight, scalars, 1 + rep + step, part_width, [], last
            )
            last[:] = [partial]
            state[g]["arrived"].append(shifted(partial, "rep", rep, step))

    def send_hidden(g):
        hidden = sums(
            state[g]["blocks"], gate_weight, up_weight, scalars, 2, part_width, state[g]["arrived"], last
        )
        last[:] = [hidden]
        state[g]["hidden"] = [hidden] + [shifted(hidden, "rep", rep, step) for step in range(1, rep)]

    def send_core(g):
        near, far, sent_near, sent_far = down_rows(
            state[g]["hidden"], down_weight, state[g]["blocks"], row_count, scalars, last
        )
        last[:] = [sent_far]
        state[g]["own"] = near, far
        state[g]["core_far"] = flipped(sent_far, ep, 1)
        state[g]["core_near"] = flipped(sent_near, ep, 1)

    def send_x(g):
        (core,) = follow(state[g]["core_far"])
        far = (state[g]["own"][1] + core.astype(F32)).astype(BF16)
        last.append(far)
        state[g]["x"] = flipped(far, ep, 2)

    def send_z(g):
        core, across = follow(state[g]["core_near"], state[g]["x"])
        near = state[g]["own"][0] + core.astype(F32) + across.astype(F32)
        near = near.reshape(per_group, 2 * row_count, width)
        state[g]["z"] = []
        for place, r in enumerate(members[g]):
            if r == 0:
                last.append(near[place])
                state[g]["z"].append(near[place])
            else:
                block = near[place].astype(BF16)
                last.append(block)
                state[g]["z"].append(flipped(block, ep, 4 * r))

    totals = []

    def finish(g):
        total = totals[-1] if totals else None
        for block in state[g]["z"]:
            total = block.astype(F32) if total is None else total + block.astype(F32)
        totals.append(total)
        last.append(total)

    def run(*turns):
        for stage, g in turns:
            stage(g)

    run((ask_x, 0), (ask_core, 0), (hold_z, 1), (send_sums, 0), (ask_x, 1), (hold_x, 1), (send_hidden, 0), (ask_core, 1))
    run((hold_z, 2), (send_sums, 1), (ask_x, 2), (send_core, 0), (hold_x, 2), (hold_z, 3), (send_hidden, 1), (send_x, 0))
    run((ask_core, 2), (send_sums, 2), (ask_x, 3), (send_core, 1), (hold_x, 3), (send_hidden, 2), (send_x, 1))
    run((ask_core, 3), (send_sums, 3), (send_core, 2), (send_z, 1), (send_x, 2), (send_hidden, 3), (send_z, 0), (finish, 0))
    run((finish, 1), (send_core, 3), (send_z, 2), (send_x, 3), (send_z, 3), (finish, 2), (finish, 3))
    total = totals[-1]
    return total[:row_count].astype(BF16), total[row_count:].astype(BF16)


def solution(mesh):
    return jax.shard_map(
        shards,
        mesh=mesh,
        in_specs=(
            P("ep", "rep"),
            P("ep", "rep"),
            P("ep", None),
            P("ep", None),
            P("ep", None),
            P("ep", None),
            P(),
            P(),
            P("ep", "rep", None),
            P("ep", "rep", None),
            P("ep", None, "rep"),
        ),
        out_specs=(P("ep", "rep"), P("ep", "rep")),
        check_vma=False,
    )
```

```python
import functools
import math

import jax
import jax.numpy as jnp
from jax import lax
from jax.experimental import pallas as pl
from jax.experimental.pallas import tpu as pltpu
from jax.sharding import PartitionSpec as P

VMEM_LIMIT = 8 * 1024 * 1024
QUICK = pl.CostEstimate(flops=1, bytes_accessed=1, transcendentals=0)
F32 = jnp.float32
BF16 = jnp.bfloat16
EXTRA = 128
PIECES = 3


def scale_of(extra, step_rows, one, two):
    values = extra.astype(F32)
    names = pltpu.roll(values, EXTRA // 2, 1)
    row = lax.broadcasted_iota(jnp.int32, values.shape, 0)
    lane = lax.broadcasted_iota(jnp.int32, values.shape, 1)
    wanted = jnp.where(row % (2 * step_rows) < step_rows, one, two).astype(F32)
    chosen = jnp.logical_and(names == wanted, lane < EXTRA // 2)
    return jnp.sum(jnp.where(chosen, values, 0.0), axis=1, keepdims=True)


def in_hbm(array):
    return pltpu.with_memory_space_constraint(array, pltpu.HBM)


def in_vmem(array):
    return pltpu.with_memory_space_constraint(array, pltpu.VMEM)


def vmem_limit(*shapes):
    return sum(2 * math.prod(shape) for shape in shapes) + 5 * 1024 * 1024


def load_kernel(count, *refs):
    sems = refs[2 * count]
    copies = [pltpu.make_async_copy(refs[i], refs[count + i], sems.at[i]) for i in range(count)]
    for copy in copies:
        copy.start()
    for copy in copies:
        copy.wait()


def load(arrays, after):
    count = len(arrays)
    any_spec = pl.BlockSpec(memory_space=pl.ANY)
    return pl.pallas_call(
        lambda *refs: load_kernel(count, *refs[:count], *refs[count + len(after) :]),
        out_shape=[pltpu.VMEM(array.shape, array.dtype) for array in arrays],
        in_specs=[any_spec] * (count + len(after)),
        out_specs=[pl.BlockSpec(memory_space=pltpu.VMEM)] * count,
        scratch_shapes=[pltpu.SemaphoreType.DMA((count,))],
        compiler_params=pltpu.CompilerParams(vmem_limit_bytes=VMEM_LIMIT),
        cost_estimate=QUICK,
    )(*[in_hbm(array) for array in arrays], *after)


def sums_kernel(block_count, arrived_count, after_count, part, scalar_ref, *refs):
    block_refs = refs[:block_count]
    gate_ref, up_ref = refs[block_count : block_count + 2]
    arrived_refs = refs[block_count + 2 : block_count + 2 + arrived_count]
    out_ref, rows = refs[block_count + 2 + arrived_count + after_count :]
    depth = rows.shape[1]
    part_width = out_ref.shape[-1]
    tile = 256 if part_width % 256 == 0 else part_width
    start = 0
    for ref in block_refs:
        rows[start : start + ref.shape[0]] = ref[:, :depth]
        start += ref.shape[0]
    for j in range(part_width // tile):
        span = pl.ds(pl.multiple_of(scalar_ref[part] * part_width + j * tile, tile), tile)
        here = slice(j * tile, (j + 1) * tile)
        gate = jnp.dot(rows[...], gate_ref[0, :, span], preferred_element_type=F32)
        up = jnp.dot(rows[...], up_ref[0, :, span], preferred_element_type=F32)
        if arrived_count == 0:
            out_ref[0, :, here] = gate.astype(BF16)
            out_ref[1, :, here] = up.astype(BF16)
        else:
            for ref in arrived_refs:
                gate = gate + ref[0, :, here].astype(F32)
                up = up + ref[1, :, here].astype(F32)
            out_ref[:, here] = (gate / (1.0 + jnp.exp(-gate)) * up).astype(BF16)


def sums(blocks, gate_weight, up_weight, scalars, part, part_width, arrived, after):
    count = sum(block.shape[0] for block in blocks)
    depth = gate_weight.shape[1]
    out_shape = (count, part_width) if arrived else (2, count, part_width)
    any_spec = pl.BlockSpec(memory_space=pl.ANY)
    vmem_spec = pl.BlockSpec(memory_space=pltpu.VMEM)
    return pl.pallas_call(
        functools.partial(sums_kernel, len(blocks), len(arrived), len(after), part),
        out_shape=jax.ShapeDtypeStruct(out_shape, BF16),
        grid_spec=pltpu.PrefetchScalarGridSpec(
            num_scalar_prefetch=1,
            grid=(),
            in_specs=[vmem_spec] * (len(blocks) + 2 + len(arrived)) + [any_spec] * len(after),
            out_specs=vmem_spec,
            scratch_shapes=[pltpu.VMEM((count, depth), BF16)],
        ),
        compiler_params=pltpu.CompilerParams(
            vmem_limit_bytes=vmem_limit(
                (count, depth), *[block.shape for block in blocks], *[pair.shape for pair in arrived], out_shape
            )
        ),
        cost_estimate=QUICK,
    )(scalars, *blocks, in_vmem(gate_weight), in_vmem(up_weight), *arrived, *after)


def down_kernel(parts, block_count, after_count, step_rows, scalar_ref, *refs):
    hidden_refs = refs[:parts]
    down_ref = refs[parts]
    block_refs = refs[parts + 1 : parts + 1 + block_count]
    near_ref, far_ref, sent_near_ref, sent_far_ref, hidden = refs[parts + 1 + block_count + after_count :]
    part_width = hidden_refs[0].shape[1]
    width = down_ref.shape[2]
    for p, ref in enumerate(hidden_refs):
        start = pl.multiple_of(scalar_ref[2 + p] * part_width, part_width)
        hidden[:, pl.ds(start, part_width)] = ref[...]
    scale = jnp.concatenate(
        [scale_of(ref[:, width:], step_rows, scalar_ref[0], scalar_ref[1]) for ref in block_refs], axis=0
    )
    quarter = scale.shape[0] // 4
    tile = 512 if width % 512 == 0 else 256
    for j in range(width // tile):
        here = slice(j * tile, (j + 1) * tile)
        total = jnp.dot(hidden[...], down_ref[0, :, here], preferred_element_type=F32) * scale
        for i, ref in enumerate((near_ref, far_ref, sent_near_ref, sent_far_ref)):
            ref[:, here] = total[i * quarter : (i + 1) * quarter].astype(ref.dtype)


def down_rows(hidden_parts, down_weight, blocks, step_rows, scalars, after):
    parts = len(hidden_parts)
    count, part_width = hidden_parts[0].shape
    width = down_weight.shape[2]
    any_spec = pl.BlockSpec(memory_space=pl.ANY)
    vmem_spec = pl.BlockSpec(memory_space=pltpu.VMEM)
    return pl.pallas_call(
        functools.partial(down_kernel, parts, len(blocks), len(after), step_rows),
        out_shape=[jax.ShapeDtypeStruct((count // 4, width), dtype) for dtype in (F32, F32, BF16, BF16)],
        grid_spec=pltpu.PrefetchScalarGridSpec(
            num_scalar_prefetch=1,
            grid=(),
            in_specs=[vmem_spec] * (parts + 1 + len(blocks)) + [any_spec] * len(after),
            out_specs=[vmem_spec] * 4,
            scratch_shapes=[pltpu.VMEM((count, parts * part_width), BF16)],
        ),
        compiler_params=pltpu.CompilerParams(
            vmem_limit_bytes=vmem_limit(
                (2 * count, parts * part_width), *[block.shape for block in blocks], (3 * count // 2, width)
            )
        ),
        cost_estimate=QUICK,
    )(scalars, *hidden_parts, in_vmem(down_weight), *blocks, *after)


def base_kernel(one_ref, two_ref, route_one_ref, route_two_ref, gate_one_ref, gate_two_ref, out_ref):
    step_rows, width = one_ref.shape
    top = route_one_ref.shape[0]
    out_ref[:step_rows, :width] = one_ref[...]
    out_ref[step_rows:, :width] = two_ref[...]
    column = lax.broadcasted_iota(jnp.int32, (top, EXTRA), 1)
    choice = lax.broadcasted_iota(jnp.int32, (top, EXTRA), 0)

    def placed(value, start):
        where = (column == choice + start).astype(BF16)
        return lax.dot_general(
            value.astype(BF16), where, (((0,), (0,)), ((), ())), preferred_element_type=F32
        )

    for place, route_ref, gate_ref in ((0, route_one_ref, gate_one_ref), (1, route_two_ref, gate_two_ref)):
        rest = gate_ref[...]
        names = route_ref[...].astype(F32)
        total = None
        for piece in range(PIECES):
            part = rest.astype(BF16).astype(F32)
            rest = rest - part
            term = placed(part, piece * top) + placed(names, EXTRA // 2 + piece * top)
            total = term if total is None else total + term
        out_ref[place * step_rows : (place + 1) * step_rows, width:] = total.astype(BF16)


def base_rows(tokens_one, tokens_two, routes_one, routes_two, gates_one, gates_two):
    step_rows, width = tokens_one.shape
    return pl.pallas_call(
        base_kernel,
        out_shape=jax.ShapeDtypeStruct((2 * step_rows, width + EXTRA), BF16),
        in_specs=[pl.BlockSpec(memory_space=pltpu.VMEM)] * 6,
        out_specs=pl.BlockSpec(memory_space=pltpu.VMEM),
        compiler_params=pltpu.CompilerParams(vmem_limit_bytes=VMEM_LIMIT),
    )(*[in_hbm(array) for array in (tokens_one, tokens_two, routes_one.T, routes_two.T, gates_one.T, gates_two.T)])


def shifted(value, axis, size, step):
    return lax.ppermute(value, axis, [(i, (i + step) % size) for i in range(size)])


def flipped(value, size, bits):
    return lax.ppermute(value, "ep", [(i, i ^ bits) for i in range(size)])


def shards(
    tokens_one,
    tokens_two,
    routes_one,
    routes_two,
    gates_one,
    gates_two,
    place_before,
    swap_flags,
    gate_weight,
    up_weight,
    down_weight,
):
    ep = lax.axis_size("ep")
    rep = lax.axis_size("rep")
    me = lax.axis_index("ep")
    y = lax.axis_index("rep")
    half = ep // 2
    z_count = ep // 4
    row_count, width = tokens_one.shape
    part_width = gate_weight.shape[2] // rep
    indices = jnp.arange(ep, dtype=jnp.int32)

    part_ids = [y] + [(y - step) % rep for step in range(1, rep)]
    turn_ids = [(y + step) % rep for step in range(1, rep)]
    expert = jnp.sum(jnp.where(place_before == me, indices, 0))
    flag = jnp.sum(jnp.where(indices[:half] == me % half, swap_flags, 0))
    after = jnp.where(flag == 1, jnp.where(me < half, me + half, me - half), me)
    scalars = jnp.stack([expert, after] + part_ids + turn_ids).astype(jnp.int32)

    both = base_rows(tokens_one, tokens_two, routes_one, routes_two, gates_one, gates_two)

    groups = 4
    per_group = z_count // groups
    members = [[group * per_group + i for i in range(per_group)] for group in (0, 2, 3, 1)]
    early = {0: both}
    for group in (members[0], members[1], members[3], members[2]):
        for r in group:
            early[r] = early.get(r) if r == 0 else flipped(both, ep, 4 * r)
    along_z = [[early[r] for r in group] for group in members]
    gate_weight, up_weight = load([gate_weight, up_weight], [both, scalars])
    (down_weight,) = load([down_weight], [gate_weight])
    state = [dict() for _ in range(groups)]
    last = [down_weight]

    def follow(*values):
        held = lax.optimization_barrier(tuple(values) + tuple(last))
        return held[: len(values)]

    def ask_x(g):
        near = along_z[g] if g == 0 else follow(*along_z[g])
        state[g]["near"] = list(near)
        state[g]["across"] = [flipped(value, ep, 2) for value in near]

    def ask_core(g):
        across = list(follow(*state[g]["across"]))
        here = state[g]["near"] + across
        state[g]["blocks"] = here + [flipped(value, ep, 1) for value in here]

    def hold_z(g):
        last.extend(along_z[g])

    def hold_x(g):
        last.extend(state[g]["across"])

    def hold_core(g):
        last.append(state[g]["core_far"])

    def send_sums(g):
        state[g]["arrived"] = []
        for step in range(1, rep):
            partial = sums(
                state[g]["blocks"], gate_weight, up_weight, scalars, 1 + rep + step, part_width, [], last
            )
            last[:] = [partial]
            state[g]["arrived"].append(shifted(partial, "rep", rep, step))

    def send_hidden(g):
        hidden = sums(
            state[g]["blocks"], gate_weight, up_weight, scalars, 2, part_width, state[g]["arrived"], last
        )
        last[:] = [hidden]
        state[g]["hidden"] = [hidden] + [shifted(hidden, "rep", rep, step) for step in range(1, rep)]

    def send_core(g):
        near, far, sent_near, sent_far = down_rows(
            state[g]["hidden"], down_weight, state[g]["blocks"], row_count, scalars, last
        )
        last[:] = [sent_far]
        state[g]["own"] = near, far
        state[g]["core_far"] = flipped(sent_far, ep, 1)
        state[g]["core_near"] = flipped(sent_near, ep, 1)

    def send_x(g):
        (core,) = follow(state[g]["core_far"])
        far = (state[g]["own"][1] + core.astype(F32)).astype(BF16)
        last.append(far)
        state[g]["x"] = flipped(far, ep, 2)

    def send_z(g):
        core, across = follow(state[g]["core_near"], state[g]["x"])
        near = state[g]["own"][0] + core.astype(F32) + across.astype(F32)
        near = near.reshape(per_group, 2 * row_count, width)
        state[g]["z"] = []
        for place, r in enumerate(members[g]):
            if r == 0:
                last.append(near[place])
                state[g]["z"].append(near[place])
            else:
                block = near[place].astype(BF16)
                last.append(block)
                state[g]["z"].append(flipped(block, ep, 4 * r))

    totals = []

    def finish(g):
        total = totals[-1] if totals else None
        for block in state[g]["z"]:
            total = block.astype(F32) if total is None else total + block.astype(F32)
        totals.append(total)
        last.append(total)

    def run(*turns):
        for stage, g in turns:
            stage(g)

    run((ask_x, 0), (ask_core, 0), (hold_z, 1), (send_sums, 0), (ask_x, 1), (hold_x, 1), (send_hidden, 0), (ask_core, 1))
    run((hold_z, 3), (hold_z, 2), (send_sums, 1), (ask_x, 2), (send_core, 0), (hold_x, 2), (send_hidden, 1), (hold_core, 0))
    run((ask_core, 2), (ask_x, 3), (send_sums, 2), (hold_x, 3), (send_core, 1), (send_hidden, 2), (send_x, 1))
    run((ask_core, 3), (send_sums, 3), (send_core, 2), (send_z, 1), (send_x, 0), (send_hidden, 3), (send_x, 2), (send_z, 0), (finish, 0))
    run((send_core, 3), (finish, 1), (send_z, 2), (send_x, 3), (send_z, 3), (finish, 2), (finish, 3))
    total = totals[-1]
    return total[:row_count].astype(BF16), total[row_count:].astype(BF16)


def solution(mesh):
    return jax.shard_map(
        shards,
        mesh=mesh,
        in_specs=(
            P("ep", "rep"),
            P("ep", "rep"),
            P("ep", None),
            P("ep", None),
            P("ep", None),
            P("ep", None),
            P(),
            P(),
            P("ep", "rep", None),
            P("ep", "rep", None),
            P("ep", None, "rep"),
        ),
        out_specs=(P("ep", "rep"), P("ep", "rep")),
        check_vma=False,
    )
```

```python
import functools
import math

import jax
import jax.numpy as jnp
from jax import lax
from jax.experimental import pallas as pl
from jax.experimental.pallas import tpu as pltpu
from jax.sharding import PartitionSpec as P

VMEM_LIMIT = 8 * 1024 * 1024
QUICK = pl.CostEstimate(flops=1, bytes_accessed=1, transcendentals=0)
F32 = jnp.float32
BF16 = jnp.bfloat16
EXTRA = 128
PIECES = 3


def scale_of(extra, step_rows, one, two):
    values = extra.astype(F32)
    names = pltpu.roll(values, EXTRA // 2, 1)
    row = lax.broadcasted_iota(jnp.int32, values.shape, 0)
    lane = lax.broadcasted_iota(jnp.int32, values.shape, 1)
    wanted = jnp.where(row % (2 * step_rows) < step_rows, one, two).astype(F32)
    chosen = jnp.logical_and(names == wanted, lane < EXTRA // 2)
    return jnp.sum(jnp.where(chosen, values, 0.0), axis=1, keepdims=True)


def in_hbm(array):
    return pltpu.with_memory_space_constraint(array, pltpu.HBM)


def in_vmem(array):
    return pltpu.with_memory_space_constraint(array, pltpu.VMEM)


def vmem_limit(*shapes):
    return sum(2 * math.prod(shape) for shape in shapes) + 5 * 1024 * 1024


def load_kernel(count, *refs):
    sems = refs[2 * count]
    copies = [pltpu.make_async_copy(refs[i], refs[count + i], sems.at[i]) for i in range(count)]
    for copy in copies:
        copy.start()
    for copy in copies:
        copy.wait()


def load(arrays, after):
    count = len(arrays)
    any_spec = pl.BlockSpec(memory_space=pl.ANY)
    return pl.pallas_call(
        lambda *refs: load_kernel(count, *refs[:count], *refs[count + len(after) :]),
        out_shape=[pltpu.VMEM(array.shape, array.dtype) for array in arrays],
        in_specs=[any_spec] * (count + len(after)),
        out_specs=[pl.BlockSpec(memory_space=pltpu.VMEM)] * count,
        scratch_shapes=[pltpu.SemaphoreType.DMA((count,))],
        compiler_params=pltpu.CompilerParams(vmem_limit_bytes=VMEM_LIMIT),
        cost_estimate=QUICK,
    )(*[in_hbm(array) for array in arrays], *after)


def sums_kernel(block_count, arrived_count, after_count, part, scalar_ref, *refs):
    block_refs = refs[:block_count]
    gate_ref, up_ref = refs[block_count : block_count + 2]
    arrived_refs = refs[block_count + 2 : block_count + 2 + arrived_count]
    out_ref, rows = refs[block_count + 2 + arrived_count + after_count :]
    depth = rows.shape[1]
    part_width = out_ref.shape[-1]
    tile = 256 if part_width % 256 == 0 else part_width
    start = 0
    for ref in block_refs:
        rows[start : start + ref.shape[0]] = ref[:, :depth]
        start += ref.shape[0]
    for j in range(part_width // tile):
        span = pl.ds(pl.multiple_of(scalar_ref[part] * part_width + j * tile, tile), tile)
        here = slice(j * tile, (j + 1) * tile)
        gate = jnp.dot(rows[...], gate_ref[0, :, span], preferred_element_type=F32)
        up = jnp.dot(rows[...], up_ref[0, :, span], preferred_element_type=F32)
        if arrived_count == 0:
            out_ref[0, :, here] = gate.astype(BF16)
            out_ref[1, :, here] = up.astype(BF16)
        else:
            for ref in arrived_refs:
                gate = gate + ref[0, :, here].astype(F32)
                up = up + ref[1, :, here].astype(F32)
            out_ref[:, here] = (gate / (1.0 + jnp.exp(-gate)) * up).astype(BF16)


def sums(blocks, gate_weight, up_weight, scalars, part, part_width, arrived, after):
    count = sum(block.shape[0] for block in blocks)
    depth = gate_weight.shape[1]
    out_shape = (count, part_width) if arrived else (2, count, part_width)
    any_spec = pl.BlockSpec(memory_space=pl.ANY)
    vmem_spec = pl.BlockSpec(memory_space=pltpu.VMEM)
    return pl.pallas_call(
        functools.partial(sums_kernel, len(blocks), len(arrived), len(after), part),
        out_shape=jax.ShapeDtypeStruct(out_shape, BF16),
        grid_spec=pltpu.PrefetchScalarGridSpec(
            num_scalar_prefetch=1,
            grid=(),
            in_specs=[vmem_spec] * (len(blocks) + 2 + len(arrived)) + [any_spec] * len(after),
            out_specs=vmem_spec,
            scratch_shapes=[pltpu.VMEM((count, depth), BF16)],
        ),
        compiler_params=pltpu.CompilerParams(
            vmem_limit_bytes=vmem_limit(
                (count, depth), *[block.shape for block in blocks], *[pair.shape for pair in arrived], out_shape
            )
        ),
        cost_estimate=QUICK,
    )(scalars, *blocks, in_vmem(gate_weight), in_vmem(up_weight), *arrived, *after)


def down_kernel(parts, block_count, after_count, step_rows, scalar_ref, *refs):
    hidden_refs = refs[:parts]
    down_ref = refs[parts]
    block_refs = refs[parts + 1 : parts + 1 + block_count]
    near_ref, far_ref, sent_near_ref, sent_far_ref, hidden = refs[parts + 1 + block_count + after_count :]
    part_width = hidden_refs[0].shape[1]
    width = down_ref.shape[2]
    for p, ref in enumerate(hidden_refs):
        start = pl.multiple_of(scalar_ref[2 + p] * part_width, part_width)
        hidden[:, pl.ds(start, part_width)] = ref[...]
    scale = jnp.concatenate(
        [scale_of(ref[:, width:], step_rows, scalar_ref[0], scalar_ref[1]) for ref in block_refs], axis=0
    )
    quarter = scale.shape[0] // 4
    tile = 512 if width % 512 == 0 else 256
    for j in range(width // tile):
        here = slice(j * tile, (j + 1) * tile)
        total = jnp.dot(hidden[...], down_ref[0, :, here], preferred_element_type=F32) * scale
        for i, ref in enumerate((near_ref, far_ref, sent_near_ref, sent_far_ref)):
            ref[:, here] = total[i * quarter : (i + 1) * quarter].astype(ref.dtype)


def down_rows(hidden_parts, down_weight, blocks, step_rows, scalars, after):
    parts = len(hidden_parts)
    count, part_width = hidden_parts[0].shape
    width = down_weight.shape[2]
    any_spec = pl.BlockSpec(memory_space=pl.ANY)
    vmem_spec = pl.BlockSpec(memory_space=pltpu.VMEM)
    return pl.pallas_call(
        functools.partial(down_kernel, parts, len(blocks), len(after), step_rows),
        out_shape=[jax.ShapeDtypeStruct((count // 4, width), dtype) for dtype in (F32, F32, BF16, BF16)],
        grid_spec=pltpu.PrefetchScalarGridSpec(
            num_scalar_prefetch=1,
            grid=(),
            in_specs=[vmem_spec] * (parts + 1 + len(blocks)) + [any_spec] * len(after),
            out_specs=[vmem_spec] * 4,
            scratch_shapes=[pltpu.VMEM((count, parts * part_width), BF16)],
        ),
        compiler_params=pltpu.CompilerParams(
            vmem_limit_bytes=vmem_limit(
                (2 * count, parts * part_width), *[block.shape for block in blocks], (3 * count // 2, width)
            )
        ),
        cost_estimate=QUICK,
    )(scalars, *hidden_parts, in_vmem(down_weight), *blocks, *after)


def base_kernel(one_ref, two_ref, route_one_ref, route_two_ref, gate_one_ref, gate_two_ref, out_ref):
    step_rows, width = one_ref.shape
    top = route_one_ref.shape[0]
    out_ref[:step_rows, :width] = one_ref[...]
    out_ref[step_rows:, :width] = two_ref[...]
    column = lax.broadcasted_iota(jnp.int32, (top, EXTRA), 1)
    choice = lax.broadcasted_iota(jnp.int32, (top, EXTRA), 0)

    def placed(value, start):
        where = (column == choice + start).astype(BF16)
        return lax.dot_general(
            value.astype(BF16), where, (((0,), (0,)), ((), ())), preferred_element_type=F32
        )

    for place, route_ref, gate_ref in ((0, route_one_ref, gate_one_ref), (1, route_two_ref, gate_two_ref)):
        rest = gate_ref[...]
        names = route_ref[...].astype(F32)
        total = None
        for piece in range(PIECES):
            part = rest.astype(BF16).astype(F32)
            rest = rest - part
            term = placed(part, piece * top) + placed(names, EXTRA // 2 + piece * top)
            total = term if total is None else total + term
        out_ref[place * step_rows : (place + 1) * step_rows, width:] = total.astype(BF16)


def base_rows(tokens_one, tokens_two, routes_one, routes_two, gates_one, gates_two):
    step_rows, width = tokens_one.shape
    return pl.pallas_call(
        base_kernel,
        out_shape=jax.ShapeDtypeStruct((2 * step_rows, width + EXTRA), BF16),
        in_specs=[pl.BlockSpec(memory_space=pltpu.VMEM)] * 6,
        out_specs=pl.BlockSpec(memory_space=pltpu.VMEM),
        compiler_params=pltpu.CompilerParams(vmem_limit_bytes=VMEM_LIMIT),
    )(*[in_hbm(array) for array in (tokens_one, tokens_two, routes_one.T, routes_two.T, gates_one.T, gates_two.T)])


def shifted(value, axis, size, step):
    return lax.ppermute(value, axis, [(i, (i + step) % size) for i in range(size)])


def flipped(value, size, bits):
    return lax.ppermute(value, "ep", [(i, i ^ bits) for i in range(size)])


def shards(
    tokens_one,
    tokens_two,
    routes_one,
    routes_two,
    gates_one,
    gates_two,
    place_before,
    swap_flags,
    gate_weight,
    up_weight,
    down_weight,
):
    ep = lax.axis_size("ep")
    rep = lax.axis_size("rep")
    me = lax.axis_index("ep")
    y = lax.axis_index("rep")
    half = ep // 2
    z_count = ep // 4
    row_count, width = tokens_one.shape
    part_width = gate_weight.shape[2] // rep
    indices = jnp.arange(ep, dtype=jnp.int32)

    part_ids = [y] + [(y - step) % rep for step in range(1, rep)]
    turn_ids = [(y + step) % rep for step in range(1, rep)]
    expert = jnp.sum(jnp.where(place_before == me, indices, 0))
    flag = jnp.sum(jnp.where(indices[:half] == me % half, swap_flags, 0))
    after = jnp.where(flag == 1, jnp.where(me < half, me + half, me - half), me)
    scalars = jnp.stack([expert, after] + part_ids + turn_ids).astype(jnp.int32)

    both = base_rows(tokens_one, tokens_two, routes_one, routes_two, gates_one, gates_two)

    groups = 4
    per_group = z_count // groups
    members = [[group * per_group + i for i in range(per_group)] for group in (0, 2, 3, 1)]
    early = {0: both}
    for group in (members[0], members[1], members[3], members[2]):
        for r in group:
            early[r] = early.get(r) if r == 0 else flipped(both, ep, 4 * r)
    along_z = [[early[r] for r in group] for group in members]
    gate_weight, up_weight = load([gate_weight, up_weight], [both, scalars])
    (down_weight,) = load([down_weight], [gate_weight])
    state = [dict() for _ in range(groups)]
    last = [down_weight]

    def follow(*values):
        held = lax.optimization_barrier(tuple(values) + tuple(last))
        return held[: len(values)]

    def ask_x(g):
        near = along_z[g] if g == 0 else follow(*along_z[g])
        state[g]["near"] = list(near)
        state[g]["across"] = [flipped(value, ep, 2) for value in near]

    def ask_core(g):
        across = list(follow(*state[g]["across"]))
        here = state[g]["near"] + across
        state[g]["blocks"] = here + [flipped(value, ep, 1) for value in here]

    def hold_z(g):
        last.extend(along_z[g])

    def hold_x(g):
        last.extend(state[g]["across"])

    def hold_core(g):
        last.append(state[g]["core_far"])

    def send_sums(g):
        state[g]["arrived"] = []
        for step in range(1, rep):
            partial = sums(
                state[g]["blocks"], gate_weight, up_weight, scalars, 1 + rep + step, part_width, [], last
            )
            last[:] = [partial]
            state[g]["arrived"].append(shifted(partial, "rep", rep, step))

    def send_hidden(g):
        hidden = sums(
            state[g]["blocks"], gate_weight, up_weight, scalars, 2, part_width, state[g]["arrived"], last
        )
        last[:] = [hidden]
        state[g]["hidden"] = [hidden] + [shifted(hidden, "rep", rep, step) for step in range(1, rep)]

    def send_core(g):
        near, far, sent_near, sent_far = down_rows(
            state[g]["hidden"], down_weight, state[g]["blocks"], row_count, scalars, last
        )
        last[:] = [sent_far]
        state[g]["own"] = near, far
        state[g]["core_far"] = flipped(sent_far, ep, 1)
        state[g]["core_near"] = flipped(sent_near, ep, 1)

    def send_x(g):
        (core,) = follow(state[g]["core_far"])
        far = (state[g]["own"][1] + core.astype(F32)).astype(BF16)
        last.append(far)
        state[g]["x"] = flipped(far, ep, 2)

    def send_z(g):
        core, across = follow(state[g]["core_near"], state[g]["x"])
        near = state[g]["own"][0] + core.astype(F32) + across.astype(F32)
        near = near.reshape(per_group, 2 * row_count, width)
        state[g]["z"] = []
        for place, r in enumerate(members[g]):
            if r == 0:
                last.append(near[place])
                state[g]["z"].append(near[place])
            else:
                block = near[place].astype(BF16)
                last.append(block)
                state[g]["z"].append(flipped(block, ep, 4 * r))

    totals = []

    def finish(g):
        total = totals[-1] if totals else None
        for block in state[g]["z"]:
            total = block.astype(F32) if total is None else total + block.astype(F32)
        totals.append(total)
        last.append(total)

    def run(*turns):
        for stage, g in turns:
            stage(g)

    run((ask_x, 0), (ask_core, 0), (hold_z, 1), (send_sums, 0), (ask_x, 1), (hold_x, 1), (send_hidden, 0), (ask_core, 1))
    run((hold_z, 2), (send_sums, 1), (ask_x, 2), (send_core, 0), (hold_x, 2), (send_hidden, 1), (hold_core, 0), (hold_z, 3))
    run((ask_core, 2), (ask_x, 3), (send_sums, 2), (hold_x, 3), (send_core, 1), (send_hidden, 2), (send_x, 1))
    run((ask_core, 3), (send_sums, 3), (send_core, 2), (send_z, 1), (send_x, 0), (send_hidden, 3), (send_x, 2))
    run((send_core, 3), (send_z, 0), (finish, 0), (finish, 1), (send_x, 3), (send_z, 2), (send_z, 3), (finish, 2), (finish, 3))
    total = totals[-1]
    return total[:row_count].astype(BF16), total[row_count:].astype(BF16)


def solution(mesh):
    return jax.shard_map(
        shards,
        mesh=mesh,
        in_specs=(
            P("ep", "rep"),
            P("ep", "rep"),
            P("ep", None),
            P("ep", None),
            P("ep", None),
            P("ep", None),
            P(),
            P(),
            P("ep", "rep", None),
            P("ep", "rep", None),
            P("ep", None, "rep"),
        ),
        out_specs=(P("ep", "rep"), P("ep", "rep")),
        check_vma=False,
    )
```

```python
import functools
import math

import jax
import jax.numpy as jnp
from jax import lax
from jax.experimental import pallas as pl
from jax.experimental.pallas import tpu as pltpu
from jax.sharding import PartitionSpec as P

VMEM_LIMIT = 8 * 1024 * 1024
QUICK = pl.CostEstimate(flops=1, bytes_accessed=1, transcendentals=0)
F32 = jnp.float32
BF16 = jnp.bfloat16
EXTRA = 128
PIECES = 3
PIECES_SENT = (2, 1, 1, 1)


def scale_of(extra, step_rows, one, two):
    values = extra.astype(F32)
    names = pltpu.roll(values, EXTRA // 2, 1)
    row = lax.broadcasted_iota(jnp.int32, values.shape, 0)
    lane = lax.broadcasted_iota(jnp.int32, values.shape, 1)
    wanted = jnp.where(row % (2 * step_rows) < step_rows, one, two).astype(F32)
    chosen = jnp.logical_and(names == wanted, lane < EXTRA // 2)
    return jnp.sum(jnp.where(chosen, values, 0.0), axis=1, keepdims=True)


def in_hbm(array):
    return pltpu.with_memory_space_constraint(array, pltpu.HBM)


def in_vmem(array):
    return pltpu.with_memory_space_constraint(array, pltpu.VMEM)


def vmem_limit(*shapes):
    return sum(2 * math.prod(shape) for shape in shapes) + 5 * 1024 * 1024


def load_kernel(count, *refs):
    sems = refs[2 * count]
    copies = [pltpu.make_async_copy(refs[i], refs[count + i], sems.at[i]) for i in range(count)]
    for copy in copies:
        copy.start()
    for copy in copies:
        copy.wait()


def load(arrays, after):
    count = len(arrays)
    any_spec = pl.BlockSpec(memory_space=pl.ANY)
    return pl.pallas_call(
        lambda *refs: load_kernel(count, *refs[:count], *refs[count + len(after) :]),
        out_shape=[pltpu.VMEM(array.shape, array.dtype) for array in arrays],
        in_specs=[any_spec] * (count + len(after)),
        out_specs=[pl.BlockSpec(memory_space=pltpu.VMEM)] * count,
        scratch_shapes=[pltpu.SemaphoreType.DMA((count,))],
        compiler_params=pltpu.CompilerParams(vmem_limit_bytes=VMEM_LIMIT),
        cost_estimate=QUICK,
    )(*[in_hbm(array) for array in arrays], *after)


def sums_kernel(block_count, arrived_count, after_count, part, pieces, scalar_ref, *refs):
    block_refs = refs[:block_count]
    gate_ref, up_ref = refs[block_count : block_count + 2]
    arrived_refs = refs[block_count + 2 : block_count + 2 + arrived_count]
    out_refs = refs[block_count + 2 + arrived_count + after_count : -1]
    rows = refs[-1]
    depth = rows.shape[1]
    part_width = out_refs[0].shape[-1]
    tile = 256 if part_width % 256 == 0 else part_width
    start = 0
    for ref in block_refs:
        rows[start : start + ref.shape[0]] = ref[:, :depth]
        start += ref.shape[0]
    for j in range(part_width // tile):
        span = pl.ds(pl.multiple_of(scalar_ref[part] * part_width + j * tile, tile), tile)
        here = slice(j * tile, (j + 1) * tile)
        gate = jnp.dot(rows[...], gate_ref[0, :, span], preferred_element_type=F32)
        up = jnp.dot(rows[...], up_ref[0, :, span], preferred_element_type=F32)
        if arrived_count == 0:
            out_refs[0][0, :, here] = gate.astype(BF16)
            out_refs[-1][2 // pieces - 1, :, here] = up.astype(BF16)
        else:
            for gate_in, up_in in zip(arrived_refs[::pieces], arrived_refs[pieces - 1 :: pieces]):
                gate = gate + gate_in[0, :, here].astype(F32)
                up = up + up_in[2 // pieces - 1, :, here].astype(F32)
            out_refs[0][:, here] = (gate / (1.0 + jnp.exp(-gate)) * up).astype(BF16)


def sums(blocks, gate_weight, up_weight, scalars, part, part_width, pieces, arrived, after):
    count = sum(block.shape[0] for block in blocks)
    depth = gate_weight.shape[1]
    outs = 1 if arrived else pieces
    out_shape = (count, part_width) if arrived else (2 // pieces, count, part_width)
    any_spec = pl.BlockSpec(memory_space=pl.ANY)
    vmem_spec = pl.BlockSpec(memory_space=pltpu.VMEM)
    return pl.pallas_call(
        functools.partial(sums_kernel, len(blocks), len(arrived), len(after), part, pieces),
        out_shape=[jax.ShapeDtypeStruct(out_shape, BF16)] * outs,
        grid_spec=pltpu.PrefetchScalarGridSpec(
            num_scalar_prefetch=1,
            grid=(),
            in_specs=[vmem_spec] * (len(blocks) + 2 + len(arrived)) + [any_spec] * len(after),
            out_specs=[vmem_spec] * outs,
            scratch_shapes=[pltpu.VMEM((count, depth), BF16)],
        ),
        compiler_params=pltpu.CompilerParams(
            vmem_limit_bytes=vmem_limit(
                (count, depth), *[block.shape for block in blocks], *[pair.shape for pair in arrived], *[out_shape] * outs
            )
        ),
        cost_estimate=QUICK,
    )(scalars, *blocks, in_vmem(gate_weight), in_vmem(up_weight), *arrived, *after)


def down_kernel(parts, block_count, after_count, step_rows, scalar_ref, *refs):
    hidden_refs = refs[:parts]
    down_ref = refs[parts]
    block_refs = refs[parts + 1 : parts + 1 + block_count]
    near_ref, far_ref, sent_near_ref, sent_far_ref, hidden = refs[parts + 1 + block_count + after_count :]
    part_width = hidden_refs[0].shape[1]
    width = down_ref.shape[2]
    for p, ref in enumerate(hidden_refs):
        start = pl.multiple_of(scalar_ref[2 + p] * part_width, part_width)
        hidden[:, pl.ds(start, part_width)] = ref[...]
    scale = jnp.concatenate(
        [scale_of(ref[:, width:], step_rows, scalar_ref[0], scalar_ref[1]) for ref in block_refs], axis=0
    )
    quarter = scale.shape[0] // 4
    tile = 512 if width % 512 == 0 else 256
    for j in range(width // tile):
        here = slice(j * tile, (j + 1) * tile)
        total = jnp.dot(hidden[...], down_ref[0, :, here], preferred_element_type=F32) * scale
        for i, ref in enumerate((near_ref, far_ref, sent_near_ref, sent_far_ref)):
            ref[:, here] = total[i * quarter : (i + 1) * quarter].astype(ref.dtype)


def down_rows(hidden_parts, down_weight, blocks, step_rows, scalars, after):
    parts = len(hidden_parts)
    count, part_width = hidden_parts[0].shape
    width = down_weight.shape[2]
    any_spec = pl.BlockSpec(memory_space=pl.ANY)
    vmem_spec = pl.BlockSpec(memory_space=pltpu.VMEM)
    return pl.pallas_call(
        functools.partial(down_kernel, parts, len(blocks), len(after), step_rows),
        out_shape=[jax.ShapeDtypeStruct((count // 4, width), dtype) for dtype in (F32, F32, BF16, BF16)],
        grid_spec=pltpu.PrefetchScalarGridSpec(
            num_scalar_prefetch=1,
            grid=(),
            in_specs=[vmem_spec] * (parts + 1 + len(blocks)) + [any_spec] * len(after),
            out_specs=[vmem_spec] * 4,
            scratch_shapes=[pltpu.VMEM((count, parts * part_width), BF16)],
        ),
        compiler_params=pltpu.CompilerParams(
            vmem_limit_bytes=vmem_limit(
                (2 * count, parts * part_width), *[block.shape for block in blocks], (3 * count // 2, width)
            )
        ),
        cost_estimate=QUICK,
    )(scalars, *hidden_parts, in_vmem(down_weight), *blocks, *after)


def base_kernel(one_ref, two_ref, route_one_ref, route_two_ref, gate_one_ref, gate_two_ref, out_ref):
    step_rows, width = one_ref.shape
    top = route_one_ref.shape[0]
    out_ref[:step_rows, :width] = one_ref[...]
    out_ref[step_rows:, :width] = two_ref[...]
    column = lax.broadcasted_iota(jnp.int32, (top, EXTRA), 1)
    choice = lax.broadcasted_iota(jnp.int32, (top, EXTRA), 0)

    def placed(value, start):
        where = (column == choice + start).astype(BF16)
        return lax.dot_general(
            value.astype(BF16), where, (((0,), (0,)), ((), ())), preferred_element_type=F32
        )

    for place, route_ref, gate_ref in ((0, route_one_ref, gate_one_ref), (1, route_two_ref, gate_two_ref)):
        rest = gate_ref[...]
        names = route_ref[...].astype(F32)
        total = None
        for piece in range(PIECES):
            part = rest.astype(BF16).astype(F32)
            rest = rest - part
            term = placed(part, piece * top) + placed(names, EXTRA // 2 + piece * top)
            total = term if total is None else total + term
        out_ref[place * step_rows : (place + 1) * step_rows, width:] = total.astype(BF16)


def base_rows(tokens_one, tokens_two, routes_one, routes_two, gates_one, gates_two):
    step_rows, width = tokens_one.shape
    return pl.pallas_call(
        base_kernel,
        out_shape=jax.ShapeDtypeStruct((2 * step_rows, width + EXTRA), BF16),
        in_specs=[pl.BlockSpec(memory_space=pltpu.VMEM)] * 6,
        out_specs=pl.BlockSpec(memory_space=pltpu.VMEM),
        compiler_params=pltpu.CompilerParams(vmem_limit_bytes=VMEM_LIMIT),
    )(*[in_hbm(array) for array in (tokens_one, tokens_two, routes_one.T, routes_two.T, gates_one.T, gates_two.T)])


def shifted(value, axis, size, step):
    return lax.ppermute(value, axis, [(i, (i + step) % size) for i in range(size)])


def flipped(value, size, bits):
    return lax.ppermute(value, "ep", [(i, i ^ bits) for i in range(size)])


def shards(
    tokens_one,
    tokens_two,
    routes_one,
    routes_two,
    gates_one,
    gates_two,
    place_before,
    swap_flags,
    gate_weight,
    up_weight,
    down_weight,
):
    ep = lax.axis_size("ep")
    rep = lax.axis_size("rep")
    me = lax.axis_index("ep")
    y = lax.axis_index("rep")
    half = ep // 2
    z_count = ep // 4
    row_count, width = tokens_one.shape
    part_width = gate_weight.shape[2] // rep
    indices = jnp.arange(ep, dtype=jnp.int32)

    part_ids = [y] + [(y - step) % rep for step in range(1, rep)]
    turn_ids = [(y + step) % rep for step in range(1, rep)]
    expert = jnp.sum(jnp.where(place_before == me, indices, 0))
    flag = jnp.sum(jnp.where(indices[:half] == me % half, swap_flags, 0))
    after = jnp.where(flag == 1, jnp.where(me < half, me + half, me - half), me)
    scalars = jnp.stack([expert, after] + part_ids + turn_ids).astype(jnp.int32)

    both = base_rows(tokens_one, tokens_two, routes_one, routes_two, gates_one, gates_two)

    groups = 4
    per_group = z_count // groups
    members = [[group * per_group + i for i in range(per_group)] for group in (0, 2, 3, 1)]
    early = {0: both}
    for group in (members[0], members[1], members[3], members[2]):
        for r in group:
            early[r] = early.get(r) if r == 0 else flipped(both, ep, 4 * r)
    along_z = [[early[r] for r in group] for group in members]
    gate_weight, up_weight = load([gate_weight, up_weight], [both, scalars])
    (down_weight,) = load([down_weight], [gate_weight])
    state = [dict() for _ in range(groups)]
    last = [down_weight]

    def follow(*values):
        held = lax.optimization_barrier(tuple(values) + tuple(last))
        return held[: len(values)]

    def ask_x(g):
        near = along_z[g] if g == 0 else follow(*along_z[g])
        state[g]["near"] = list(near)
        state[g]["across"] = [flipped(value, ep, 2) for value in near]

    def ask_core(g):
        across = list(follow(*state[g]["across"]))
        here = state[g]["near"] + across
        state[g]["blocks"] = here + [flipped(value, ep, 1) for value in here]

    def hold_z(g):
        last.extend(along_z[g])

    def hold_x(g):
        last.extend(state[g]["across"])

    def hold_blocks(g):
        last.extend(state[g]["blocks"])

    def hold_core(g):
        last.append(state[g]["core_far"])

    def send_sums(g):
        state[g]["arrived"] = []
        for step in range(1, rep):
            partial = sums(
                state[g]["blocks"], gate_weight, up_weight, scalars, 1 + rep + step, part_width, PIECES_SENT[g], [], last
            )
            last[:] = [partial[-1]]
            state[g]["arrived"] += [shifted(value, "rep", rep, step) for value in partial]

    def send_hidden(g):
        (hidden,) = sums(
            state[g]["blocks"], gate_weight, up_weight, scalars, 2, part_width, PIECES_SENT[g], state[g]["arrived"], last
        )
        last[:] = [hidden]
        state[g]["hidden"] = [hidden] + [shifted(hidden, "rep", rep, step) for step in range(1, rep)]

    def send_core(g):
        near, far, sent_near, sent_far = down_rows(
            state[g]["hidden"], down_weight, state[g]["blocks"], row_count, scalars, last
        )
        last[:] = [sent_far]
        state[g]["own"] = near, far
        state[g]["core_far"] = flipped(sent_far, ep, 1)
        state[g]["core_near"] = flipped(sent_near, ep, 1)

    def send_x(g):
        (core,) = follow(state[g]["core_far"])
        far = (state[g]["own"][1] + core.astype(F32)).astype(BF16)
        last.append(far)
        state[g]["x"] = flipped(far, ep, 2)

    def send_z(g):
        core, across = follow(state[g]["core_near"], state[g]["x"])
        near = state[g]["own"][0] + core.astype(F32) + across.astype(F32)
        near = near.reshape(per_group, 2 * row_count, width)
        state[g]["z"] = []
        for place, r in enumerate(members[g]):
            if r == 0:
                last.append(near[place])
                state[g]["z"].append(near[place])
            else:
                block = near[place].astype(BF16)
                last.append(block)
                state[g]["z"].append(flipped(block, ep, 4 * r))

    totals = []

    def finish(g):
        total = totals[-1] if totals else None
        for block in state[g]["z"]:
            total = block.astype(F32) if total is None else total + block.astype(F32)
        totals.append(total)
        last.append(total)

    def run(*turns):
        for stage, g in turns:
            stage(g)

    run((ask_x, 0), (hold_z, 1), (ask_core, 0), (ask_x, 1), (send_sums, 0), (hold_x, 1), (send_hidden, 0), (hold_z, 2), (ask_core, 1))
    run((send_sums, 1), (ask_x, 2), (send_core, 0), (hold_x, 2), (send_hidden, 1), (hold_core, 0), (hold_z, 3))
    run((ask_core, 2), (ask_x, 3), (send_sums, 2), (hold_x, 3), (send_core, 1), (send_hidden, 2), (send_x, 1))
    run((ask_core, 3), (send_sums, 3), (send_core, 2), (send_z, 1), (send_x, 0), (send_hidden, 3), (send_x, 2))
    run((send_core, 3), (send_z, 0), (finish, 0), (finish, 1), (send_x, 3), (send_z, 2), (send_z, 3), (finish, 2), (finish, 3))
    total = totals[-1]
    return total[:row_count].astype(BF16), total[row_count:].astype(BF16)


def solution(mesh):
    return jax.shard_map(
        shards,
        mesh=mesh,
        in_specs=(
            P("ep", "rep"),
            P("ep", "rep"),
            P("ep", None),
            P("ep", None),
            P("ep", None),
            P("ep", None),
            P(),
            P(),
            P("ep", "rep", None),
            P("ep", "rep", None),
            P("ep", None, "rep"),
        ),
        out_specs=(P("ep", "rep"), P("ep", "rep")),
        check_vma=False,
    )
```

```python
import functools
import math

import jax
import jax.numpy as jnp
from jax import lax
from jax.experimental import pallas as pl
from jax.experimental.pallas import tpu as pltpu
from jax.sharding import PartitionSpec as P

VMEM_LIMIT = 8 * 1024 * 1024
QUICK = pl.CostEstimate(flops=1, bytes_accessed=1, transcendentals=0)
F32 = jnp.float32
BF16 = jnp.bfloat16
EXTRA = 128
PIECES = 3


def scale_of(extra, step_rows, one, two):
    values = extra.astype(F32)
    names = pltpu.roll(values, EXTRA // 2, 1)
    row = lax.broadcasted_iota(jnp.int32, values.shape, 0)
    lane = lax.broadcasted_iota(jnp.int32, values.shape, 1)
    wanted = jnp.where(row % (2 * step_rows) < step_rows, one, two).astype(F32)
    chosen = jnp.logical_and(names == wanted, lane < EXTRA // 2)
    return jnp.sum(jnp.where(chosen, values, 0.0), axis=1, keepdims=True)


def in_hbm(array):
    return pltpu.with_memory_space_constraint(array, pltpu.HBM)


def in_vmem(array):
    return pltpu.with_memory_space_constraint(array, pltpu.VMEM)


def vmem_limit(*shapes):
    return sum(2 * math.prod(shape) for shape in shapes) + 5 * 1024 * 1024


def load_kernel(count, *refs):
    sems = refs[2 * count]
    copies = [pltpu.make_async_copy(refs[i], refs[count + i], sems.at[i]) for i in range(count)]
    for copy in copies:
        copy.start()
    for copy in copies:
        copy.wait()


def load(arrays, after):
    count = len(arrays)
    any_spec = pl.BlockSpec(memory_space=pl.ANY)
    return pl.pallas_call(
        lambda *refs: load_kernel(count, *refs[:count], *refs[count + len(after) :]),
        out_shape=[pltpu.VMEM(array.shape, array.dtype) for array in arrays],
        in_specs=[any_spec] * (count + len(after)),
        out_specs=[pl.BlockSpec(memory_space=pltpu.VMEM)] * count,
        scratch_shapes=[pltpu.SemaphoreType.DMA((count,))],
        compiler_params=pltpu.CompilerParams(vmem_limit_bytes=VMEM_LIMIT),
        cost_estimate=QUICK,
    )(*[in_hbm(array) for array in arrays], *after)


def sums_kernel(block_count, arrived_count, after_count, part, scalar_ref, *refs):
    block_refs = refs[:block_count]
    gate_ref, up_ref = refs[block_count : block_count + 2]
    arrived_refs = refs[block_count + 2 : block_count + 2 + arrived_count]
    out_ref, rows = refs[block_count + 2 + arrived_count + after_count :]
    depth = rows.shape[1]
    part_width = out_ref.shape[-1]
    tile = 256 if part_width % 256 == 0 else part_width
    start = 0
    for ref in block_refs:
        rows[start : start + ref.shape[0]] = ref[:, :depth]
        start += ref.shape[0]
    for j in range(part_width // tile):
        span = pl.ds(pl.multiple_of(scalar_ref[part] * part_width + j * tile, tile), tile)
        here = slice(j * tile, (j + 1) * tile)
        gate = jnp.dot(rows[...], gate_ref[0, :, span], preferred_element_type=F32)
        up = jnp.dot(rows[...], up_ref[0, :, span], preferred_element_type=F32)
        if arrived_count == 0:
            out_ref[0, :, here] = gate.astype(BF16)
            out_ref[1, :, here] = up.astype(BF16)
        else:
            for ref in arrived_refs:
                gate = gate + ref[0, :, here].astype(F32)
                up = up + ref[1, :, here].astype(F32)
            out_ref[:, here] = (gate / (1.0 + jnp.exp(-gate)) * up).astype(BF16)


def sums(blocks, gate_weight, up_weight, scalars, part, part_width, arrived, after):
    count = sum(block.shape[0] for block in blocks)
    depth = gate_weight.shape[1]
    out_shape = (count, part_width) if arrived else (2, count, part_width)
    any_spec = pl.BlockSpec(memory_space=pl.ANY)
    vmem_spec = pl.BlockSpec(memory_space=pltpu.VMEM)
    return pl.pallas_call(
        functools.partial(sums_kernel, len(blocks), len(arrived), len(after), part),
        out_shape=jax.ShapeDtypeStruct(out_shape, BF16),
        grid_spec=pltpu.PrefetchScalarGridSpec(
            num_scalar_prefetch=1,
            grid=(),
            in_specs=[vmem_spec] * (len(blocks) + 2 + len(arrived)) + [any_spec] * len(after),
            out_specs=vmem_spec,
            scratch_shapes=[pltpu.VMEM((count, depth), BF16)],
        ),
        compiler_params=pltpu.CompilerParams(
            vmem_limit_bytes=vmem_limit(
                (count, depth), *[block.shape for block in blocks], *[pair.shape for pair in arrived], out_shape
            )
        ),
        cost_estimate=QUICK,
    )(scalars, *blocks, in_vmem(gate_weight), in_vmem(up_weight), *arrived, *after)


def down_kernel(parts, block_count, after_count, step_rows, scalar_ref, *refs):
    hidden_refs = refs[:parts]
    down_ref = refs[parts]
    block_refs = refs[parts + 1 : parts + 1 + block_count]
    near_ref, far_ref, sent_near_ref, sent_far_ref, hidden = refs[parts + 1 + block_count + after_count :]
    part_width = hidden_refs[0].shape[1]
    width = down_ref.shape[2]
    for p, ref in enumerate(hidden_refs):
        start = pl.multiple_of(scalar_ref[2 + p] * part_width, part_width)
        hidden[:, pl.ds(start, part_width)] = ref[...]
    scale = jnp.concatenate(
        [scale_of(ref[:, width:], step_rows, scalar_ref[0], scalar_ref[1]) for ref in block_refs], axis=0
    )
    quarter = scale.shape[0] // 4
    tile = 512 if width % 512 == 0 else 256
    for j in range(width // tile):
        here = slice(j * tile, (j + 1) * tile)
        total = jnp.dot(hidden[...], down_ref[0, :, here], preferred_element_type=F32) * scale
        for i, ref in enumerate((near_ref, far_ref, sent_near_ref, sent_far_ref)):
            ref[:, here] = total[i * quarter : (i + 1) * quarter].astype(ref.dtype)


def down_rows(hidden_parts, down_weight, blocks, step_rows, scalars, after):
    parts = len(hidden_parts)
    count, part_width = hidden_parts[0].shape
    width = down_weight.shape[2]
    any_spec = pl.BlockSpec(memory_space=pl.ANY)
    vmem_spec = pl.BlockSpec(memory_space=pltpu.VMEM)
    return pl.pallas_call(
        functools.partial(down_kernel, parts, len(blocks), len(after), step_rows),
        out_shape=[jax.ShapeDtypeStruct((count // 4, width), dtype) for dtype in (F32, F32, BF16, BF16)],
        grid_spec=pltpu.PrefetchScalarGridSpec(
            num_scalar_prefetch=1,
            grid=(),
            in_specs=[vmem_spec] * (parts + 1 + len(blocks)) + [any_spec] * len(after),
            out_specs=[vmem_spec] * 4,
            scratch_shapes=[pltpu.VMEM((count, parts * part_width), BF16)],
        ),
        compiler_params=pltpu.CompilerParams(
            vmem_limit_bytes=vmem_limit(
                (2 * count, parts * part_width), *[block.shape for block in blocks], (3 * count // 2, width)
            )
        ),
        cost_estimate=QUICK,
    )(scalars, *hidden_parts, in_vmem(down_weight), *blocks, *after)


def base_kernel(one_ref, two_ref, route_one_ref, route_two_ref, gate_one_ref, gate_two_ref, out_ref):
    step_rows, width = one_ref.shape
    top = route_one_ref.shape[0]
    out_ref[:step_rows, :width] = one_ref[...]
    out_ref[step_rows:, :width] = two_ref[...]
    column = lax.broadcasted_iota(jnp.int32, (top, EXTRA), 1)
    choice = lax.broadcasted_iota(jnp.int32, (top, EXTRA), 0)

    def placed(value, start):
        where = (column == choice + start).astype(BF16)
        return lax.dot_general(
            value.astype(BF16), where, (((0,), (0,)), ((), ())), preferred_element_type=F32
        )

    for place, route_ref, gate_ref in ((0, route_one_ref, gate_one_ref), (1, route_two_ref, gate_two_ref)):
        rest = gate_ref[...]
        names = route_ref[...].astype(F32)
        total = None
        for piece in range(PIECES):
            part = rest.astype(BF16).astype(F32)
            rest = rest - part
            term = placed(part, piece * top) + placed(names, EXTRA // 2 + piece * top)
            total = term if total is None else total + term
        out_ref[place * step_rows : (place + 1) * step_rows, width:] = total.astype(BF16)


def base_rows(tokens_one, tokens_two, routes_one, routes_two, gates_one, gates_two):
    step_rows, width = tokens_one.shape
    return pl.pallas_call(
        base_kernel,
        out_shape=jax.ShapeDtypeStruct((2 * step_rows, width + EXTRA), BF16),
        in_specs=[pl.BlockSpec(memory_space=pltpu.VMEM)] * 6,
        out_specs=pl.BlockSpec(memory_space=pltpu.VMEM),
        compiler_params=pltpu.CompilerParams(vmem_limit_bytes=VMEM_LIMIT),
    )(*[in_hbm(array) for array in (tokens_one, tokens_two, routes_one.T, routes_two.T, gates_one.T, gates_two.T)])


def shifted(value, axis, size, step):
    return lax.ppermute(value, axis, [(i, (i + step) % size) for i in range(size)])


def flipped(value, size, bits):
    return lax.ppermute(value, "ep", [(i, i ^ bits) for i in range(size)])


def shards(
    tokens_one,
    tokens_two,
    routes_one,
    routes_two,
    gates_one,
    gates_two,
    place_before,
    swap_flags,
    gate_weight,
    up_weight,
    down_weight,
):
    ep = lax.axis_size("ep")
    rep = lax.axis_size("rep")
    me = lax.axis_index("ep")
    y = lax.axis_index("rep")
    half = ep // 2
    z_count = ep // 4
    row_count, width = tokens_one.shape
    part_width = gate_weight.shape[2] // rep
    indices = jnp.arange(ep, dtype=jnp.int32)

    part_ids = [y] + [(y - step) % rep for step in range(1, rep)]
    turn_ids = [(y + step) % rep for step in range(1, rep)]
    expert = jnp.sum(jnp.where(place_before == me, indices, 0))
    flag = jnp.sum(jnp.where(indices[:half] == me % half, swap_flags, 0))
    after = jnp.where(flag == 1, jnp.where(me < half, me + half, me - half), me)
    scalars = jnp.stack([expert, after] + part_ids + turn_ids).astype(jnp.int32)

    both = base_rows(tokens_one, tokens_two, routes_one, routes_two, gates_one, gates_two)

    groups = 4
    per_group = z_count // groups
    members = [[group * per_group + i for i in range(per_group)] for group in (0, 2, 3, 1)]
    along_z = [[both if r == 0 else flipped(both, ep, 4 * r) for r in members[g]] for g in (0, 1, 3)]
    along_z.insert(2, [flipped(value, ep, 4 * per_group) for value in along_z[1]])
    gate_weight, up_weight = load([gate_weight, up_weight], [both, scalars])
    (down_weight,) = load([down_weight], [gate_weight])
    state = [dict() for _ in range(groups)]
    last = [down_weight]

    def follow(*values):
        held = lax.optimization_barrier(tuple(values) + tuple(last))
        return held[: len(values)]

    def ask_x(g):
        near = along_z[g] if g == 0 else follow(*along_z[g])
        state[g]["near"] = list(near)
        state[g]["across"] = [flipped(value, ep, 2) for value in near]

    def ask_core(g):
        across = list(follow(*state[g]["across"]))
        here = state[g]["near"] + across
        state[g]["blocks"] = here + [flipped(value, ep, 1) for value in here]

    def hold_z(g):
        last.extend(along_z[g])

    def hold_x(g):
        last.extend(state[g]["across"])

    def hold_blocks(g):
        last.extend(state[g]["blocks"])

    def hold_core(g):
        last.append(state[g]["core_far"])

    def send_sums(g):
        state[g]["arrived"] = []
        for step in range(1, rep):
            partial = sums(
                state[g]["blocks"], gate_weight, up_weight, scalars, 1 + rep + step, part_width, [], last
            )
            last[:] = [partial]
            state[g]["arrived"].append(shifted(partial, "rep", rep, step))

    def send_hidden(g):
        hidden = sums(
            state[g]["blocks"], gate_weight, up_weight, scalars, 2, part_width, state[g]["arrived"], last
        )
        last[:] = [hidden]
        state[g]["hidden"] = [hidden] + [shifted(hidden, "rep", rep, step) for step in range(1, rep)]

    def send_core(g):
        near, far, sent_near, sent_far = down_rows(
            state[g]["hidden"], down_weight, state[g]["blocks"], row_count, scalars, last
        )
        last[:] = [sent_far]
        state[g]["own"] = near, far
        state[g]["core_far"] = flipped(sent_far, ep, 1)
        state[g]["core_near"] = flipped(sent_near, ep, 1)

    def send_x(g):
        (core,) = follow(state[g]["core_far"])
        far = (state[g]["own"][1] + core.astype(F32)).astype(BF16)
        last.append(far)
        state[g]["x"] = flipped(far, ep, 2)

    def send_z(g):
        core, across = follow(state[g]["core_near"], state[g]["x"])
        near = state[g]["own"][0] + core.astype(F32) + across.astype(F32)
        near = near.reshape(per_group, 2 * row_count, width)
        state[g]["z"] = []
        for place, r in enumerate(members[g]):
            if r == 0:
                last.append(near[place])
                state[g]["z"].append(near[place])
            else:
                block = near[place].astype(BF16)
                last.append(block)
                state[g]["z"].append(flipped(block, ep, 4 * r))

    totals = []

    def finish(g):
        total = totals[-1] if totals else None
        for block in state[g]["z"]:
            total = block.astype(F32) if total is None else total + block.astype(F32)
        totals.append(total)
        last.append(total)

    def run(*turns):
        for stage, g in turns:
            stage(g)

    run((ask_x, 0), (ask_core, 0), (hold_z, 3), (hold_z, 1), (send_sums, 0), (ask_x, 1), (hold_x, 1), (send_hidden, 0), (hold_z, 2), (ask_core, 1), (ask_x, 2))
    run((send_sums, 1), (send_core, 0), (hold_x, 2), (send_hidden, 1), (hold_core, 0), (ask_core, 2), (ask_x, 3))
    run((send_sums, 2), (hold_x, 3), (send_core, 1), (send_hidden, 2), (send_x, 1), (ask_core, 3), (send_sums, 3))
    run((send_core, 2), (send_z, 1), (send_x, 0), (send_hidden, 3), (send_x, 2))
    run((send_core, 3), (send_z, 0), (finish, 0), (finish, 1), (send_x, 3), (send_z, 2), (send_z, 3), (finish, 2), (finish, 3))
    total = totals[-1]
    return total[:row_count].astype(BF16), total[row_count:].astype(BF16)


def solution(mesh):
    return jax.shard_map(
        shards,
        mesh=mesh,
        in_specs=(
            P("ep", "rep"),
            P("ep", "rep"),
            P("ep", None),
            P("ep", None),
            P("ep", None),
            P("ep", None),
            P(),
            P(),
            P("ep", "rep", None),
            P("ep", "rep", None),
            P("ep", None, "rep"),
        ),
        out_specs=(P("ep", "rep"), P("ep", "rep")),
        check_vma=False,
    )
```

```python
import functools
import math

import jax
import jax.numpy as jnp
from jax import lax
from jax.experimental import pallas as pl
from jax.experimental.pallas import tpu as pltpu
from jax.sharding import PartitionSpec as P

VMEM_LIMIT = 8 * 1024 * 1024
QUICK = pl.CostEstimate(flops=1, bytes_accessed=1, transcendentals=0)
F32 = jnp.float32
BF16 = jnp.bfloat16
EXTRA = 128
PIECES = 3


def scale_of(extra, step_rows, one, two):
    values = extra.astype(F32)
    names = pltpu.roll(values, EXTRA // 2, 1)
    row = lax.broadcasted_iota(jnp.int32, values.shape, 0)
    lane = lax.broadcasted_iota(jnp.int32, values.shape, 1)
    wanted = jnp.where(row % (2 * step_rows) < step_rows, one, two).astype(F32)
    chosen = jnp.logical_and(names == wanted, lane < EXTRA // 2)
    return jnp.sum(jnp.where(chosen, values, 0.0), axis=1, keepdims=True)


def in_hbm(array):
    return pltpu.with_memory_space_constraint(array, pltpu.HBM)


def in_vmem(array):
    return pltpu.with_memory_space_constraint(array, pltpu.VMEM)


def vmem_limit(*shapes):
    return sum(2 * math.prod(shape) for shape in shapes) + 5 * 1024 * 1024


def load_kernel(count, *refs):
    sems = refs[2 * count]
    copies = [pltpu.make_async_copy(refs[i], refs[count + i], sems.at[i]) for i in range(count)]
    for copy in copies:
        copy.start()
    for copy in copies:
        copy.wait()


def load(arrays, after):
    count = len(arrays)
    any_spec = pl.BlockSpec(memory_space=pl.ANY)
    return pl.pallas_call(
        lambda *refs: load_kernel(count, *refs[:count], *refs[count + len(after) :]),
        out_shape=[pltpu.VMEM(array.shape, array.dtype) for array in arrays],
        in_specs=[any_spec] * (count + len(after)),
        out_specs=[pl.BlockSpec(memory_space=pltpu.VMEM)] * count,
        scratch_shapes=[pltpu.SemaphoreType.DMA((count,))],
        compiler_params=pltpu.CompilerParams(vmem_limit_bytes=VMEM_LIMIT),
        cost_estimate=QUICK,
    )(*[in_hbm(array) for array in arrays], *after)


def sums_kernel(block_count, arrived_count, after_count, part, scalar_ref, *refs):
    block_refs = refs[:block_count]
    gate_ref, up_ref = refs[block_count : block_count + 2]
    arrived_refs = refs[block_count + 2 : block_count + 2 + arrived_count]
    out_ref, rows = refs[block_count + 2 + arrived_count + after_count :]
    depth = rows.shape[1]
    part_width = out_ref.shape[-1]
    tile = 256 if part_width % 256 == 0 else part_width
    start = 0
    for ref in block_refs:
        rows[start : start + ref.shape[0]] = ref[:, :depth]
        start += ref.shape[0]
    for j in range(part_width // tile):
        span = pl.ds(pl.multiple_of(scalar_ref[part] * part_width + j * tile, tile), tile)
        here = slice(j * tile, (j + 1) * tile)
        gate = jnp.dot(rows[...], gate_ref[0, :, span], preferred_element_type=F32)
        up = jnp.dot(rows[...], up_ref[0, :, span], preferred_element_type=F32)
        if arrived_count == 0:
            out_ref[0, :, here] = gate.astype(BF16)
            out_ref[1, :, here] = up.astype(BF16)
        else:
            for ref in arrived_refs:
                gate = gate + ref[0, :, here].astype(F32)
                up = up + ref[1, :, here].astype(F32)
            out_ref[:, here] = (gate / (1.0 + jnp.exp(-gate)) * up).astype(BF16)


def sums(blocks, gate_weight, up_weight, scalars, part, part_width, arrived, after):
    count = sum(block.shape[0] for block in blocks)
    depth = gate_weight.shape[1]
    out_shape = (count, part_width) if arrived else (2, count, part_width)
    any_spec = pl.BlockSpec(memory_space=pl.ANY)
    vmem_spec = pl.BlockSpec(memory_space=pltpu.VMEM)
    return pl.pallas_call(
        functools.partial(sums_kernel, len(blocks), len(arrived), len(after), part),
        out_shape=jax.ShapeDtypeStruct(out_shape, BF16),
        grid_spec=pltpu.PrefetchScalarGridSpec(
            num_scalar_prefetch=1,
            grid=(),
            in_specs=[vmem_spec] * (len(blocks) + 2 + len(arrived)) + [any_spec] * len(after),
            out_specs=vmem_spec,
            scratch_shapes=[pltpu.VMEM((count, depth), BF16)],
        ),
        compiler_params=pltpu.CompilerParams(
            vmem_limit_bytes=vmem_limit(
                (count, depth), *[block.shape for block in blocks], *[pair.shape for pair in arrived], out_shape
            )
        ),
        cost_estimate=QUICK,
    )(scalars, *blocks, in_vmem(gate_weight), in_vmem(up_weight), *arrived, *after)


def down_kernel(parts, block_count, after_count, step_rows, scalar_ref, *refs):
    hidden_refs = refs[:parts]
    down_ref = refs[parts]
    block_refs = refs[parts + 1 : parts + 1 + block_count]
    near_ref, far_ref, sent_near_ref, sent_far_ref, hidden = refs[parts + 1 + block_count + after_count :]
    part_width = hidden_refs[0].shape[1]
    width = down_ref.shape[2]
    for p, ref in enumerate(hidden_refs):
        start = pl.multiple_of(scalar_ref[2 + p] * part_width, part_width)
        hidden[:, pl.ds(start, part_width)] = ref[...]
    scale = jnp.concatenate(
        [scale_of(ref[:, width:], step_rows, scalar_ref[0], scalar_ref[1]) for ref in block_refs], axis=0
    )
    quarter = scale.shape[0] // 4
    tile = 512 if width % 512 == 0 else 256
    for j in range(width // tile):
        here = slice(j * tile, (j + 1) * tile)
        total = jnp.dot(hidden[...], down_ref[0, :, here], preferred_element_type=F32) * scale
        for i, ref in enumerate((near_ref, far_ref, sent_near_ref, sent_far_ref)):
            ref[:, here] = total[i * quarter : (i + 1) * quarter].astype(ref.dtype)


def down_rows(hidden_parts, down_weight, blocks, step_rows, scalars, after):
    parts = len(hidden_parts)
    count, part_width = hidden_parts[0].shape
    width = down_weight.shape[2]
    any_spec = pl.BlockSpec(memory_space=pl.ANY)
    vmem_spec = pl.BlockSpec(memory_space=pltpu.VMEM)
    return pl.pallas_call(
        functools.partial(down_kernel, parts, len(blocks), len(after), step_rows),
        out_shape=[jax.ShapeDtypeStruct((count // 4, width), dtype) for dtype in (F32, F32, BF16, BF16)],
        grid_spec=pltpu.PrefetchScalarGridSpec(
            num_scalar_prefetch=1,
            grid=(),
            in_specs=[vmem_spec] * (parts + 1 + len(blocks)) + [any_spec] * len(after),
            out_specs=[vmem_spec] * 4,
            scratch_shapes=[pltpu.VMEM((count, parts * part_width), BF16)],
        ),
        compiler_params=pltpu.CompilerParams(
            vmem_limit_bytes=vmem_limit(
                (2 * count, parts * part_width), *[block.shape for block in blocks], (3 * count // 2, width)
            )
        ),
        cost_estimate=QUICK,
    )(scalars, *hidden_parts, in_vmem(down_weight), *blocks, *after)


def base_kernel(one_ref, two_ref, route_one_ref, route_two_ref, gate_one_ref, gate_two_ref, out_ref):
    step_rows, width = one_ref.shape
    top = route_one_ref.shape[0]
    out_ref[:step_rows, :width] = one_ref[...]
    out_ref[step_rows:, :width] = two_ref[...]
    column = lax.broadcasted_iota(jnp.int32, (top, EXTRA), 1)
    choice = lax.broadcasted_iota(jnp.int32, (top, EXTRA), 0)

    def placed(value, start):
        where = (column == choice + start).astype(BF16)
        return lax.dot_general(
            value.astype(BF16), where, (((0,), (0,)), ((), ())), preferred_element_type=F32
        )

    for place, route_ref, gate_ref in ((0, route_one_ref, gate_one_ref), (1, route_two_ref, gate_two_ref)):
        rest = gate_ref[...]
        names = route_ref[...].astype(F32)
        total = None
        for piece in range(PIECES):
            part = rest.astype(BF16).astype(F32)
            rest = rest - part
            term = placed(part, piece * top) + placed(names, EXTRA // 2 + piece * top)
            total = term if total is None else total + term
        out_ref[place * step_rows : (place + 1) * step_rows, width:] = total.astype(BF16)


def base_rows(tokens_one, tokens_two, routes_one, routes_two, gates_one, gates_two):
    step_rows, width = tokens_one.shape
    return pl.pallas_call(
        base_kernel,
        out_shape=jax.ShapeDtypeStruct((2 * step_rows, width + EXTRA), BF16),
        in_specs=[pl.BlockSpec(memory_space=pltpu.VMEM)] * 6,
        out_specs=pl.BlockSpec(memory_space=pltpu.VMEM),
        compiler_params=pltpu.CompilerParams(vmem_limit_bytes=VMEM_LIMIT),
    )(*[in_hbm(array) for array in (tokens_one, tokens_two, routes_one.T, routes_two.T, gates_one.T, gates_two.T)])


def shifted(value, axis, size, step):
    return lax.ppermute(value, axis, [(i, (i + step) % size) for i in range(size)])


def flipped(value, size, bits):
    return lax.ppermute(value, "ep", [(i, i ^ bits) for i in range(size)])


def shards(
    tokens_one,
    tokens_two,
    routes_one,
    routes_two,
    gates_one,
    gates_two,
    place_before,
    swap_flags,
    gate_weight,
    up_weight,
    down_weight,
):
    ep = lax.axis_size("ep")
    rep = lax.axis_size("rep")
    me = lax.axis_index("ep")
    y = lax.axis_index("rep")
    half = ep // 2
    z_count = ep // 4
    row_count, width = tokens_one.shape
    part_width = gate_weight.shape[2] // rep
    indices = jnp.arange(ep, dtype=jnp.int32)

    part_ids = [y] + [(y - step) % rep for step in range(1, rep)]
    turn_ids = [(y + step) % rep for step in range(1, rep)]
    expert = jnp.sum(jnp.where(place_before == me, indices, 0))
    flag = jnp.sum(jnp.where(indices[:half] == me % half, swap_flags, 0))
    after = jnp.where(flag == 1, jnp.where(me < half, me + half, me - half), me)
    scalars = jnp.stack([expert, after] + part_ids + turn_ids).astype(jnp.int32)

    both = base_rows(tokens_one, tokens_two, routes_one, routes_two, gates_one, gates_two)

    groups = 4
    per_group = z_count // groups
    members = [[group * per_group + i for i in range(per_group)] for group in (0, 2, 3, 1)]
    along_z = [[both if r == 0 else flipped(both, ep, 4 * r) for r in members[g]] for g in (0, 1, 3)]
    along_z.insert(2, [flipped(value, ep, 4 * per_group) for value in along_z[1]])
    gate_weight, up_weight = load([gate_weight, up_weight], [both, scalars])
    (down_weight,) = load([down_weight], [gate_weight])
    state = [dict() for _ in range(groups)]
    last = [down_weight]

    def follow(*values):
        held = lax.optimization_barrier(tuple(values) + tuple(last))
        return held[: len(values)]

    def ask_x(g):
        near = along_z[g] if g == 0 else follow(*along_z[g])
        state[g]["near"] = list(near)
        state[g]["across"] = [flipped(value, ep, 2) for value in near]

    def ask_core(g):
        across = list(follow(*state[g]["across"]))
        here = state[g]["near"] + across
        state[g]["blocks"] = here + [flipped(value, ep, 1) for value in here]

    def hold_z(g):
        last.extend(along_z[g])

    def hold_x(g):
        last.extend(state[g]["across"])

    def hold_blocks(g):
        last.extend(state[g]["blocks"])

    def hold_core(g):
        last.append(state[g]["core_far"])

    def send_sums(g):
        state[g]["arrived"] = []
        for step in range(1, rep):
            partial = sums(
                state[g]["blocks"], gate_weight, up_weight, scalars, 1 + rep + step, part_width, [], last
            )
            last[:] = [partial]
            state[g]["arrived"].append(shifted(partial, "rep", rep, step))

    def send_hidden(g):
        hidden = sums(
            state[g]["blocks"], gate_weight, up_weight, scalars, 2, part_width, state[g]["arrived"], last
        )
        last[:] = [hidden]
        state[g]["hidden"] = [hidden] + [shifted(hidden, "rep", rep, step) for step in range(1, rep)]

    def send_core(g):
        near, far, sent_near, sent_far = down_rows(
            state[g]["hidden"], down_weight, state[g]["blocks"], row_count, scalars, last
        )
        last[:] = [sent_far]
        state[g]["own"] = near, far
        state[g]["core_far"] = flipped(sent_far, ep, 1)
        state[g]["core_near"] = flipped(sent_near, ep, 1)

    def send_x(g):
        (core,) = follow(state[g]["core_far"])
        far = (state[g]["own"][1] + core.astype(F32)).astype(BF16)
        last.append(far)
        state[g]["x"] = flipped(far, ep, 2)

    def send_z(g):
        core, across = follow(state[g]["core_near"], state[g]["x"])
        near = state[g]["own"][0] + core.astype(F32) + across.astype(F32)
        near = near.reshape(per_group, 2 * row_count, width)
        state[g]["z"] = []
        for place, r in enumerate(members[g]):
            if r == 0:
                last.append(near[place])
                state[g]["z"].append(near[place])
            else:
                block = near[place].astype(BF16)
                last.append(block)
                state[g]["z"].append(flipped(block, ep, 4 * r))

    totals = []

    def finish(g):
        total = totals[-1] if totals else None
        for block in state[g]["z"]:
            total = block.astype(F32) if total is None else total + block.astype(F32)
        totals.append(total)
        last.append(total)

    def run(*turns):
        for stage, g in turns:
            stage(g)

    run((ask_x, 0), (ask_core, 0), (hold_z, 3), (hold_z, 1), (send_sums, 0), (ask_x, 1), (hold_x, 1), (send_hidden, 0), (hold_z, 2), (ask_core, 1), (ask_x, 2))
    run((send_sums, 1), (send_core, 0), (hold_x, 2), (send_hidden, 1), (hold_core, 0), (ask_core, 2), (ask_x, 3))
    run((send_sums, 2), (hold_x, 3), (send_core, 1), (send_hidden, 2), (send_x, 1), (ask_core, 3), (send_sums, 3))
    run((send_core, 2), (send_z, 1), (send_x, 2), (send_hidden, 3), (send_z, 2), (send_core, 3), (finish, 1), (send_x, 3))
    run((send_x, 0), (send_z, 3), (finish, 2), (send_z, 0), (finish, 0), (finish, 3))
    total = totals[-1]
    return total[:row_count].astype(BF16), total[row_count:].astype(BF16)


def solution(mesh):
    return jax.shard_map(
        shards,
        mesh=mesh,
        in_specs=(
            P("ep", "rep"),
            P("ep", "rep"),
            P("ep", None),
            P("ep", None),
            P("ep", None),
            P("ep", None),
            P(),
            P(),
            P("ep", "rep", None),
            P("ep", "rep", None),
            P("ep", None, "rep"),
        ),
        out_specs=(P("ep", "rep"), P("ep", "rep")),
        check_vma=False,
    )
```
